32 devices in a mesh: region: 4 (over y, core), head: 8 (over z, x).
Axes of the slice: x: 2, y: 2, z: 4, core: 2. Of those that a mesh axis runs over, the one named last changes fastest.
Arguments:
- tokens: bfloat16 [8192, 4, 1024], P(('region', 'head')), may hold values from -6 to 6
- input_weight: bfloat16 [1024, 3072], replicated, may hold values from -1 to 1
- output_weight: bfloat16 [1024, 1024], replicated, may hold values from -0.1875 to 0.1875
- neighbours: int32 [64, 8], replicated, may hold values from 0 to 63, as said below
- degree: int32 [64], replicated, may hold values from 1 to 8, as said below
Outputs:
- spatial_out: bfloat16 [8192, 4, 1024], P(('region', 'head'))
The draws below stay inside these ranges and needn't reach their ends.
Inputs may be any that keep to these rules, and one draw needn't show every extreme that they name: `neighbours`: slot 0 of every block's list names the block itself. For any two different regions (blocks r * 16 to (r + 1) * 16 - 1 form region r), the distinct blocks of the one named anywhere in the lists of the other's blocks number at most 4, and exactly 4 for some pairs of regions in every draw. `degree`: some block has all 8 slots live.
All inputs are finite; a program needn't handle non-finite values.
Results may differ from the reference program's by a relative error of at most 0.014.
Values may be sent and summed in bfloat16 or wider, within the bound.
No kernel may reach another device: no remote copies, remote signals or barrier semaphores. Data moves between devices by JAX's collectives and lax.ppermute only.
A program may use at most 192 MiB of HBM per device.

```python
import math
import jax
import jax.numpy as jnp
from jax import lax

D = 1024
HEADS = 16
HEAD_SIZE = 64
BLOCK = 128
SLOTS = 8
BORDER = 4
STEPS = 4
BLK_REG = 16
SEGS = 8192
BLOCKS = 64


def draw_tokens(key, part):
    values = jnp.clip(jax.random.normal(jax.random.fold_in(key, 45), (SEGS, STEPS, D), jnp.float32), -6.0, 6.0)
    return values.astype(jnp.bfloat16)


def draw_input_weight(key, part):
    base = jnp.clip(jax.random.normal(jax.random.fold_in(key, 51), (D, 3 * D), jnp.float32), -6.0, 6.0) * D ** (-0.5)
    return base.astype(jnp.bfloat16)


def draw_neighbours(key, part):
    regions = BLOCKS // BLK_REG
    blocks = jnp.arange(BLOCKS, dtype=jnp.int32)
    home = blocks // BLK_REG
    place = blocks % BLK_REG
    noise = jax.random.randint(jax.random.fold_in(key, 11), (regions, regions, BLK_REG), 0, 1 << 20)
    noise = noise * BLK_REG + jnp.arange(BLK_REG, dtype=jnp.int32)
    ordering = jnp.argsort(noise, axis=-1).astype(jnp.int32)
    border = ordering[:, :, :BORDER]
    is_remote = jax.random.randint(jax.random.fold_in(key, 12), (BLOCKS, SLOTS), 0, 8) < 3
    source = (home[:, None] + 1 + jax.random.randint(jax.random.fold_in(key, 13), (BLOCKS, SLOTS), 0, regions - 1)) % regions
    which = jax.random.randint(jax.random.fold_in(key, 14), (BLOCKS, SLOTS), 0, BORDER)
    homes = jnp.broadcast_to(home[:, None], (BLOCKS, SLOTS))
    remote_ids = source * BLK_REG + border[source, homes, which]
    local_ids = homes * BLK_REG + jax.random.randint(jax.random.fold_in(key, 15), (BLOCKS, SLOTS), 0, BLK_REG)
    lists = jnp.where(is_remote, remote_ids, local_ids)
    forced_source = (home + 1) % regions
    forced = forced_source * BLK_REG + border[forced_source, home, jnp.minimum(place, BORDER - 1)]
    last_slot = jnp.where(place < BORDER, forced, lists[:, SLOTS - 1])
    lists = lists.at[:, SLOTS - 1].set(last_slot)
    lists = lists.at[:, 0].set(blocks)
    return lists.astype(jnp.int32)


def draw_degree(key, part):
    regions = BLOCKS // BLK_REG
    blocks = jnp.arange(BLOCKS, dtype=jnp.int32)
    home = blocks // BLK_REG
    reach = jax.random.randint(jax.random.fold_in(key, 21), (regions,), 2, SLOTS + 1)
    live = 1 + jax.random.randint(jax.random.fold_in(key, 22), (BLOCKS,), 0, reach[home])
    live = live.at[0].set(SLOTS)
    return live.astype(jnp.int32)


def bell_draw(own_key, shape, spread, most, kind=jnp.bfloat16):
    drawn = spread * jax.random.normal(own_key, shape, jnp.float32)
    return jnp.clip(drawn, min=-most, max=most).astype(kind)


def setup_inputs(seed: int = 0) -> dict:
    splits = jax.random.split(jax.random.key(seed), 6)
    return {
        "tokens": draw_tokens(jax.random.fold_in(splits[5], 71), 0),
        "input_weight": draw_input_weight(jax.random.fold_in(splits[5], 71), 0),
        "output_weight": bell_draw(splits[2], (D, D), D ** -0.5, 0.1875),
        "neighbours": draw_neighbours(jax.random.fold_in(splits[5], 71), 0),
        "degree": draw_degree(jax.random.fold_in(splits[5], 71), 0),
    }


def attend_group(queries, key_values, slot_blocks, live_count):
    gathered = key_values[slot_blocks]
    key_part = gathered[..., :HEAD_SIZE].astype(jnp.float32)
    value_part = gathered[..., HEAD_SIZE:].astype(jnp.float32)
    score_scale = HEAD_SIZE ** -0.5
    scores = jnp.einsum("gqthd,gskthd->gthqsk", queries.astype(jnp.float32), key_part) * score_scale
    live_slot = jnp.arange(SLOTS, dtype=jnp.int32)[None, :] < live_count[:, None]
    scores = jnp.where(live_slot[:, None, None, None, :, None], scores, -jnp.inf)
    row_max = jnp.max(scores, axis=(4, 5), keepdims=True)
    exponent = jnp.exp(scores - row_max)
    row_sum = jnp.sum(exponent, axis=(4, 5), keepdims=True)
    weights = (exponent / row_sum).astype(jnp.bfloat16)
    result = jnp.einsum("gthqsk,gskthd->gqthd", weights.astype(jnp.float32), value_part)
    return result.astype(jnp.bfloat16)


def reference(tokens, input_weight, output_weight, neighbours, degree):
    token_rows = tokens.reshape(SEGS * STEPS, D)
    projected = jnp.dot(token_rows, input_weight, preferred_element_type=jnp.float32).astype(jnp.bfloat16)
    projected = projected.reshape(BLOCKS, BLOCK, STEPS, HEADS, 3, HEAD_SIZE)
    queries = projected[..., 0, :]
    key_values = projected[..., 1:, :].reshape(BLOCKS, BLOCK, STEPS, HEADS, 2 * HEAD_SIZE)
    group_size = math.gcd(BLOCKS, 4)
    turn_count = BLOCKS // group_size
    query_groups = queries.reshape(turn_count, group_size, BLOCK, STEPS, HEADS, HEAD_SIZE)
    slot_groups = neighbours.reshape(turn_count, group_size, SLOTS)
    count_groups = degree.reshape(turn_count, group_size)

    def per_group(inputs):
        return attend_group(inputs[0], key_values, inputs[1], inputs[2])

    attended = lax.map(per_group, (query_groups, slot_groups, count_groups))
    attended = attended.reshape(SEGS * STEPS, D)
    result = jnp.dot(attended, output_weight, preferred_element_type=jnp.float32).astype(jnp.bfloat16)
    return result.reshape(SEGS, STEPS, D)
```

```python
import functools

import jax
import jax.numpy as jnp
from jax import lax
from jax.experimental import pallas as pl
from jax.experimental.pallas import tpu as pltpu
from jax.sharding import PartitionSpec as P

HEADS = 16
HEAD_SIZE = 64
BLOCK = 128
SLOTS = 8
BORDER = 4
CHUNKS = 2
PAIR = 2 * HEAD_SIZE


def attention_kernel(
    slot_ref, live_ref, q_ref, w_ref, *refs
):
    tables = refs[:CHUNKS]
    out_ref = refs[CHUNKS]
    kv_buf, att_buf, sems = refs[CHUNKS + 1 :]
    group = q_ref.shape[0]
    width = q_ref.shape[2]
    rows = BLOCK // CHUNKS
    scale = HEAD_SIZE ** (-0.5)

    def copy(block, slot, part):
        return pltpu.make_async_copy(
            tables[part].at[slot_ref[block, slot]],
            kv_buf.at[block, slot, pl.ds(part * rows, rows), :],
            sems.at[block, slot, part],
        )

    for block in range(group):
        for slot in range(SLOTS):

            @pl.when(slot < live_ref[block])
            def _():
                for part in range(CHUNKS):
                    copy(block, slot, part).start()

    lane = lax.broadcasted_iota(jnp.int32, (BLOCK, PAIR), 1)
    first = lane < HEAD_SIZE

    def attend(block, live):
        def one_pair(pair, carry):
            columns = pl.ds(pl.multiple_of(pair * PAIR, PAIR), PAIR)
            values_at = pl.ds(pl.multiple_of(width + pair * PAIR, PAIR), PAIR)
            q = q_ref[block, :, columns]
            zero = jnp.zeros_like(q)
            q_two = jnp.concatenate([jnp.where(first, q, zero), jnp.where(first, zero, q)], axis=0)
            keys = kv_buf[block, :live, :, columns].reshape(live * BLOCK, PAIR)
            values = kv_buf[block, :live, :, values_at].reshape(live * BLOCK, PAIR)
            scores = lax.dot_general(
                q_two, keys, (((1,), (1,)), ((), ())), preferred_element_type=jnp.float32
            )
            scores = scores * scale
            top = jnp.max(scores, axis=1, keepdims=True)
            exponent = jnp.exp(scores - top)
            total = jnp.sum(exponent, axis=1, keepdims=True)
            mixed = jnp.dot(
                exponent.astype(jnp.bfloat16), values, preferred_element_type=jnp.float32
            )
            mixed = mixed / total
            att_buf[block, :, columns] = jnp.where(
                first, mixed[:BLOCK], mixed[BLOCK:]
            ).astype(jnp.bfloat16)
            return carry

        lax.fori_loop(0, width // PAIR, one_pair, 0)

    for block in range(group):
        for slot in range(SLOTS):

            @pl.when(slot < live_ref[block])
            def _():
                for part in range(CHUNKS):
                    copy(block, slot, part).wait()

        for live in range(1, SLOTS + 1):

            @pl.when(live_ref[block] == live)
            def _():
                attend(block, live)

    flat = att_buf[...].reshape(group * BLOCK, width)
    out_ref[...] = (
        jnp.dot(flat, w_ref[...], preferred_element_type=jnp.float32)
        .astype(jnp.bfloat16)
        .reshape(group, BLOCK, width)
    )


def attention(queries, tables, slots, live, output_weight):
    group, _, width = queries.shape
    vmem = pl.BlockSpec(memory_space=pltpu.VMEM)
    smem = pl.BlockSpec(memory_space=pltpu.SMEM)
    anywhere = pl.BlockSpec(memory_space=pl.ANY)
    return pl.pallas_call(
        attention_kernel,
        out_shape=jax.ShapeDtypeStruct((group, BLOCK, width), jnp.bfloat16),
        in_specs=[smem, smem, vmem, vmem] + [anywhere] * CHUNKS,
        out_specs=vmem,
        scratch_shapes=[
            pltpu.VMEM((group, SLOTS, BLOCK, 2 * width), jnp.bfloat16),
            pltpu.VMEM((group, BLOCK, width), jnp.bfloat16),
            pltpu.SemaphoreType.DMA((group, SLOTS, CHUNKS)),
        ],
        compiler_params=pltpu.CompilerParams(vmem_limit_bytes=40 * 1024 * 1024),
        cost_estimate=pl.CostEstimate(
            flops=group * SLOTS * BLOCK * BLOCK * width * 8,
            bytes_accessed=group * SLOTS * BLOCK * width * 4,
            transcendentals=group * SLOTS * BLOCK * BLOCK * HEADS,
        ),
        name="attention",
    )(slots, live, queries, output_weight, *tables)


def shards(tokens, input_weight, output_weight, neighbours, degree):
    seg_dev, step_count, model_width = tokens.shape
    heads_here = lax.axis_size("head")
    regions = lax.axis_size("region")
    head_index = lax.axis_index("head")
    region_index = lax.axis_index("region")
    across = heads_here // step_count
    z = head_index // across
    x = head_index % across
    dev_blocks = seg_dev // BLOCK
    column_blocks = dev_blocks * step_count
    region_blocks = dev_blocks * heads_here
    rows = BLOCK // CHUNKS

    def z_move(piece, k):
        return lax.ppermute(
            piece, "head", [(i, i ^ (k * across)) for i in range(heads_here)]
        )

    def x_move(piece, k):
        return lax.ppermute(piece, "head", [(i, i ^ k) for i in range(heads_here)])

    def region_move(piece, k):
        return lax.ppermute(piece, "region", [(i, i ^ k) for i in range(regions)])

    local = jnp.arange(region_blocks, dtype=jnp.int32)
    owner = local // dev_blocks
    place = (
        ((owner % across) ^ x) * column_blocks
        + ((owner // across) ^ z) * dev_blocks
        + local % dev_blocks
    )
    own_blocks = region_index * region_blocks + local
    block_lists = neighbours.reshape(regions, region_blocks * SLOTS)
    named_by = jnp.any(block_lists[:, :, None] == own_blocks[None, None, :], axis=1)
    named_rank = jnp.cumsum(named_by.astype(jnp.int32), axis=1) - 1
    chosen = named_by[:, None, :] & (
        named_rank[:, None, :] == jnp.arange(BORDER, dtype=jnp.int32)[None, :, None]
    )
    source_place = jnp.sum(jnp.where(chosen, place[None, None, :], 0), axis=2)
    own_lists = lax.dynamic_slice_in_dim(neighbours, region_index * region_blocks, region_blocks, 0)
    own_degree = lax.dynamic_slice_in_dim(degree, region_index * region_blocks, region_blocks, 0)
    everything = jnp.arange(regions * region_blocks, dtype=jnp.int32)
    onehot = own_lists[:, :, None] == everything[None, None, :]
    wanted = jnp.any(onehot, axis=(0, 1))
    wanted_rank = (
        jnp.cumsum(wanted.reshape(regions, region_blocks).astype(jnp.int32), axis=1) - 1
    )
    source = jnp.arange(regions, dtype=jnp.int32) ^ region_index
    remote_place = region_blocks + (source[:, None] - 1) * BORDER + wanted_rank
    all_places = jnp.where(source[:, None] == 0, place[None, :], remote_place).reshape(-1)
    table_index = jnp.sum(jnp.where(onehot, all_places[None, None, :], 0), axis=2)

    weight = input_weight.reshape(model_width, HEADS, 3, HEAD_SIZE)
    weight = jnp.transpose(weight, (0, 2, 1, 3)).reshape(model_width, 3 * model_width)
    q_weight = weight[:, :model_width]
    kv_weight = weight[:, model_width:]

    by_step = jnp.transpose(
        tokens.reshape(dev_blocks, CHUNKS, rows, step_count, model_width), (3, 1, 0, 2, 4)
    )
    query_parts = []
    tables = []
    for part in range(CHUNKS):
        column = []
        for k in range(step_count):
            piece = lax.dynamic_index_in_dim(by_step[:, part], z ^ k, 0, keepdims=False)
            column.append(z_move(piece, k) if k else piece)
        pieces = list(column)
        for k in range(1, across):
            pieces += [x_move(piece, k) for piece in column]
        own = jnp.concatenate(pieces, axis=0)
        query_parts.append(jnp.dot(
            jnp.concatenate(column, axis=0).reshape(-1, model_width), q_weight,
            preferred_element_type=jnp.float32,
        ).astype(jnp.bfloat16).reshape(column_blocks, rows, model_width))
        for k in range(1, regions):
            places = lax.dynamic_index_in_dim(source_place, region_index ^ k, 0, keepdims=False)
            outgoing = jnp.concatenate(
                [lax.dynamic_slice_in_dim(own, places[i], 1, 0) for i in range(BORDER)], axis=0
            )
            pieces.append(region_move(outgoing, k))
        everything_here = jnp.concatenate(pieces, axis=0)
        table = jnp.dot(
            everything_here.reshape(-1, model_width), kv_weight, preferred_element_type=jnp.float32
        ).astype(jnp.bfloat16)
        tables.append(table.reshape(-1, rows, 2 * model_width))
    queries = jnp.stack(query_parts, axis=1).reshape(column_blocks, BLOCK, model_width)

    back = [None] * step_count
    for k in reversed(range(step_count)):
        first = ((z ^ k) * across + x) * dev_blocks
        slots = lax.dynamic_slice_in_dim(table_index, first, dev_blocks, 0)
        live = lax.dynamic_slice_in_dim(own_degree, first, dev_blocks, 0)
        result = attention(
            queries[k * dev_blocks : (k + 1) * dev_blocks], tables, slots, live, output_weight
        )
        back[k] = z_move(result, k) if k else result
    for bit in range((step_count - 1).bit_length()):
        swap = (z >> bit) & 1
        back = [
            jnp.where(swap == 1, back[k ^ (1 << bit)], back[k]) for k in range(step_count)
        ]
    return jnp.stack(
        [piece.reshape(seg_dev, model_width) for piece in back], axis=1
    )


def solution(mesh):
    in_specs = (P(("region", "head"), None, None), P(), P(), P(), P())
    out_specs = P(("region", "head"), None, None)
    return jax.shard_map(shards, mesh=mesh, in_specs=in_specs, out_specs=out_specs, check_vma=False)
```

```python
import functools

import jax
import jax.numpy as jnp
from jax import lax
from jax.experimental import pallas as pl
from jax.experimental.pallas import tpu as pltpu
from jax.sharding import PartitionSpec as P

HEADS = 16
HEAD_SIZE = 64
BLOCK = 128
SLOTS = 8
BORDER = 4
CHUNKS = 4
ROWS = BLOCK // CHUNKS
PAIR = 2 * HEAD_SIZE
UNROLL = 4
TILE = 512
MIB = 1024 * 1024
MEDIUM = pl.CostEstimate(flops=5 * 10**8, bytes_accessed=15 * 10**5, transcendentals=0)
SMALL = pl.CostEstimate(flops=1000, bytes_accessed=1000, transcendentals=0)

VMEM = pl.BlockSpec(memory_space=pltpu.VMEM)
SMEM = pl.BlockSpec(memory_space=pltpu.SMEM)
HBM = pl.BlockSpec(memory_space=pltpu.HBM)


def weight_kernel(in_ref, out_ref):
    rows, columns = out_ref.shape
    width = columns // 3
    low = lax.broadcasted_iota(jnp.int32, (rows, PAIR), 1) < HEAD_SIZE
    for pair in range(width // PAIR):
        one = in_ref[:, 3 * pair * PAIR : (3 * pair + 1) * PAIR]
        two = in_ref[:, (3 * pair + 1) * PAIR : (3 * pair + 2) * PAIR]
        three = in_ref[:, (3 * pair + 2) * PAIR : (3 * pair + 3) * PAIR]
        keys = jnp.concatenate([one[:, HEAD_SIZE:], three[:, :HEAD_SIZE]], axis=1)
        for number, value in enumerate(
            (keys, jnp.where(low, two, three), jnp.where(low, one, two))
        ):
            first = number * width + pair * PAIR
            out_ref[:, first : first + PAIR] = value


def sort_weight(weight):
    depth, columns = weight.shape
    rows = 128
    return pl.pallas_call(
        weight_kernel,
        grid=(depth // rows,),
        out_shape=jax.ShapeDtypeStruct((depth, columns), weight.dtype),
        in_specs=[pl.BlockSpec((rows, columns), lambda i: (i, 0))],
        out_specs=pl.BlockSpec((rows, columns), lambda i: (i, 0)),
        compiler_params=pltpu.CompilerParams(vmem_limit_bytes=8 * MIB),
        cost_estimate=SMALL,
        name="sort_weight",
    )(weight)


def index_kernel(
    across, dev_blocks, step_count, where_ref, list_ref, degree_ref,
    place_ref, slot_ref, live_ref, mark_ref, rank_ref,
):
    region, z, x = where_ref[0], where_ref[1], where_ref[2]
    blocks = list_ref.shape[0]
    region_blocks = across * dev_blocks * step_count
    column_blocks = dev_blocks * step_count
    regions = blocks // region_blocks

    def home(local):
        owner = local // dev_blocks
        return (
            ((owner % across) ^ x) * column_blocks
            + ((owner // across) ^ z) * dev_blocks
            + local % dev_blocks
        )

    def clear(i, carry):
        mark_ref[i] = 0
        rank_ref[i] = 0
        return carry

    lax.fori_loop(0, blocks, clear, 0)

    def look(block, carry):
        namer = block // region_blocks
        for slot in range(SLOTS):
            name = list_ref[block, slot]
            named_region = name // region_blocks

            @pl.when(named_region == region)
            def _():
                mark_ref[namer * region_blocks + name % region_blocks] = 1

            @pl.when(namer == region)
            def _():
                rank_ref[name] = 1

        return carry

    lax.fori_loop(0, blocks, look, 0)

    def clear_places(i, carry):
        place_ref[i] = 0
        return carry

    lax.fori_loop(0, (regions - 1) * BORDER, clear_places, 0)

    def ranks(k, carry):
        other = region ^ k

        def one(local, counts):
            sent, got = counts
            marked = mark_ref[other * region_blocks + local]

            @pl.when((marked == 1) & (sent < BORDER))
            def _():
                place_ref[(k - 1) * BORDER + jnp.minimum(sent, BORDER - 1)] = home(local)

            named = rank_ref[other * region_blocks + local]
            rank_ref[other * region_blocks + local] = got
            return sent + marked, got + named

        lax.fori_loop(0, region_blocks, one, (0, 0))
        return carry

    lax.fori_loop(1, regions, ranks, 0)

    def lists(i, carry):
        local = (((i // dev_blocks) ^ z) * across + x) * dev_blocks + i % dev_blocks
        block = region * region_blocks + local
        live_ref[i] = degree_ref[block]
        for slot in range(SLOTS):
            name = list_ref[block, slot]
            source = (name // region_blocks) ^ region
            direct = (source // 2 - 1) * BORDER
            handed = (regions // 2 - 1 + source // 2) * BORDER
            remote = region_blocks + jnp.where(source % 2 == 0, direct, handed) + rank_ref[name]
            slot_ref[i, slot] = jnp.where(source == 0, home(name % region_blocks), remote)
        return carry

    lax.fori_loop(0, column_blocks, lists, 0)


def find_indices(where, neighbours, degree, across, dev_blocks, step_count):
    blocks = neighbours.shape[0]
    region_blocks = across * dev_blocks * step_count
    regions = blocks // region_blocks
    column_blocks = dev_blocks * step_count
    return pl.pallas_call(
        functools.partial(index_kernel, across, dev_blocks, step_count),
        out_shape=[
            jax.ShapeDtypeStruct(((regions - 1) * BORDER,), jnp.int32),
            jax.ShapeDtypeStruct((column_blocks, SLOTS), jnp.int32),
            jax.ShapeDtypeStruct((column_blocks,), jnp.int32),
        ],
        in_specs=[SMEM] * 3,
        out_specs=[SMEM] * 3,
        scratch_shapes=[pltpu.SMEM((blocks,), jnp.int32), pltpu.SMEM((blocks,), jnp.int32)],
        compiler_params=pltpu.CompilerParams(vmem_limit_bytes=1 * MIB),
        cost_estimate=SMALL,
        name="find_indices",
    )(where, neighbours, degree)


def project_kernel(counts, kv_tiles, has_queries, *refs):
    total = sum(counts)
    weight_ref = refs[total]
    flat = refs[-1]
    outs = refs[: len(refs) - 1]
    query_rows = 0
    if has_queries:
        q_ref = outs[-1]
        outs = outs[:-1]
        query_rows = q_ref.shape[0] * q_ref.shape[1]
    outs = outs[len(outs) - len(counts) :]

    @pl.when(pl.program_id(0) == 0)
    def _():
        first = 0
        for piece in refs[:total]:
            rows = piece.shape[0] * piece.shape[1]
            flat[first : first + rows] = piece[...].reshape(rows, piece.shape[2])
            first += rows

    @pl.when(pl.program_id(0) < kv_tiles)
    def _():
        first = 0
        result = jnp.dot(flat[...], weight_ref[...], preferred_element_type=jnp.float32)
        for out_ref in outs:
            rows = out_ref.shape[0] * out_ref.shape[1]
            out_ref[...] = (
                result[first : first + rows].astype(out_ref.dtype).reshape(out_ref.shape)
            )
            first += rows

    if has_queries:

        @pl.when(pl.program_id(0) >= kv_tiles)
        def _():
            q_ref[...] = (
                jnp.dot(
                    flat[:query_rows], weight_ref[...], preferred_element_type=jnp.float32
                )
                .astype(q_ref.dtype)
                .reshape(q_ref.shape)
            )


def project(weight, groups, query=None):
    depth, columns = weight.shape
    width = columns // 3
    kv_tiles = 2 * width // TILE
    tiles = kv_tiles + (width // TILE if query else 0)
    operands, in_specs, aliases = [], [], {}
    out_shape, out_specs, counts = [], [], []
    all_rows = 0
    for pieces, table, part in groups:
        blocks = sum(piece.shape[0] for piece in pieces)
        operands += pieces
        in_specs += [pl.BlockSpec(piece.shape, lambda i: (0, 0, 0)) for piece in pieces]
        counts.append(len(pieces))
        rows = pieces[0].shape[1]
        all_rows += blocks * rows
        out_shape.append(pltpu.HBM((blocks, BLOCK, 2 * width), jnp.bfloat16))
        out_specs.append(
            pl.BlockSpec(
                (blocks, rows, TILE),
                functools.partial(lambda p, i: (0, p, jnp.minimum(i, kv_tiles - 1)), part),
            )
        )
    old = [table for _, table, _ in groups]
    if query:
        table, part = query
        blocks, rows = groups[0][0][0].shape[:2]
        old.append(table)
        out_shape.append(pltpu.HBM((blocks, BLOCK, width), jnp.bfloat16))
        out_specs.append(
            pl.BlockSpec(
                (blocks, rows, TILE),
                functools.partial(lambda p, i: (0, p, jnp.maximum(i - kv_tiles, 0)), part),
            )
        )
    operands.append(weight)
    in_specs.append(pl.BlockSpec((depth, TILE), lambda i: (0, i)))
    for number, table in enumerate(old):
        if table is not None:
            aliases[len(operands)] = number
            operands.append(table)
            in_specs.append(HBM)
    return pl.pallas_call(
        functools.partial(project_kernel, tuple(counts), kv_tiles, query is not None),
        grid=(tiles,),
        out_shape=out_shape,
        in_specs=in_specs,
        out_specs=out_specs,
        scratch_shapes=[pltpu.VMEM((all_rows, depth), jnp.bfloat16)],
        input_output_aliases=aliases,
        compiler_params=pltpu.CompilerParams(vmem_limit_bytes=24 * MIB),
        cost_estimate=SMALL,
        name="project",
    )(*operands)


def pick_kernel(count, place_ref, *refs):
    pieces = refs[:count]
    part_blocks = pieces[0].shape[0]
    item = 0
    for out_ref in refs[count:]:
        for here in range(out_ref.shape[0]):
            place = place_ref[item]
            item += 1
            for index, piece in enumerate(pieces):

                @pl.when(place // part_blocks == index)
                def _():
                    out_ref[here] = piece[place % part_blocks]


def pick(places, pieces, regions):
    counts = [BORDER] + [2 * BORDER] * (regions // 2 - 1)
    return pl.pallas_call(
        functools.partial(pick_kernel, len(pieces)),
        out_shape=[
            jax.ShapeDtypeStruct((count,) + pieces[0].shape[1:], pieces[0].dtype)
            for count in counts
        ],
        in_specs=[SMEM] + [VMEM] * len(pieces),
        out_specs=[VMEM] * len(counts),
        compiler_params=pltpu.CompilerParams(vmem_limit_bytes=8 * MIB),
        cost_estimate=SMALL,
        name="pick",
    )(places, *pieces)


def attention_kernel(
    start, count, slot_ref, live_ref, q_table, w_hbm, *refs
):
    tables = refs[:count]
    out_ref, q_buf, w_buf, kv_buf, att_buf, kv_sems, sems = refs[count:]
    group, _, width = out_ref.shape
    scale = HEAD_SIZE ** (-0.5)

    q_copy = pltpu.make_async_copy(q_table.at[pl.ds(start, group)], q_buf, sems.at[0])
    w_copy = pltpu.make_async_copy(w_hbm, w_buf, sems.at[1])
    q_copy.start()

    def each(block, action):
        def one(slot, carry):
            place = slot_ref[start + block, slot]

            first = 0
            for table in tables:
                blocks = table.shape[0]
                local = place - first

                @pl.when((local >= 0) & (local < blocks))
                def _():
                    copy = pltpu.make_async_copy(
                        table.at[jnp.clip(local, 0, blocks - 1)],
                        kv_buf.at[block, slot], kv_sems.at[block, slot],
                    )
                    if action == "start":
                        copy.start()
                    else:
                        copy.wait()

                first += blocks

            return carry

        lax.fori_loop(0, live_ref[start + block], one, 0)

    for block in range(group):
        each(block, "start")
    w_copy.start()
    q_copy.wait()

    first = lax.broadcasted_iota(jnp.int32, (BLOCK, PAIR), 1) < HEAD_SIZE

    def one_pair(block, live, pair):
        columns = pl.ds(pl.multiple_of(pair * PAIR, PAIR), PAIR)
        values_at = pl.ds(pl.multiple_of(width + pair * PAIR, PAIR), PAIR)
        q = q_buf[block, :, columns]
        zero = jnp.zeros_like(q)
        q_two = jnp.concatenate([jnp.where(first, q, zero), jnp.where(first, zero, q)], axis=0)
        keys = kv_buf[block, :live, :, columns].reshape(live * BLOCK, PAIR)
        values = kv_buf[block, :live, :, values_at].reshape(live * BLOCK, PAIR)
        scores = lax.dot_general(
            q_two, keys, (((1,), (1,)), ((), ())), preferred_element_type=jnp.float32
        )
        scores = scores * scale
        top = jnp.max(scores, axis=1, keepdims=True)
        exponent = jnp.exp(scores - top)
        total = jnp.sum(exponent, axis=1, keepdims=True)
        mixed = jnp.dot(
            exponent.astype(jnp.bfloat16), values, preferred_element_type=jnp.float32
        )
        mixed = mixed / total
        att_buf[block, :, columns] = jnp.where(
            first, mixed[:BLOCK], mixed[BLOCK:]
        ).astype(jnp.bfloat16)

    def one_block(block, carry):
        each(block, "wait")
        for live in range(1, SLOTS + 1):

            @pl.when(live_ref[start + block] == live)
            def _():
                def some_pairs(i, c):
                    for u in range(UNROLL):
                        one_pair(block, live, i * UNROLL + u)
                    return c

                lax.fori_loop(0, width // PAIR // UNROLL, some_pairs, 0)

        return carry

    lax.fori_loop(0, group, one_block, 0)

    w_copy.wait()
    flat = att_buf[...].reshape(group * BLOCK, width)
    out_ref[...] = (
        jnp.dot(flat, w_buf[...], preferred_element_type=jnp.float32)
        .astype(jnp.bfloat16)
        .reshape(group, BLOCK, width)
    )


def attention(start, group, slots, live, queries, output_weight, tables):
    width = queries.shape[2]
    return pl.pallas_call(
        functools.partial(attention_kernel, start, len(tables)),
        out_shape=jax.ShapeDtypeStruct((group, BLOCK, width), jnp.bfloat16),
        in_specs=[SMEM, SMEM] + [HBM] * (2 + len(tables)),
        out_specs=VMEM,
        scratch_shapes=[
            pltpu.VMEM((group, BLOCK, width), jnp.bfloat16),
            pltpu.VMEM(output_weight.shape, jnp.bfloat16),
            pltpu.VMEM((group, SLOTS, BLOCK, 2 * width), jnp.bfloat16),
            pltpu.VMEM((group, BLOCK, width), jnp.bfloat16),
            pltpu.SemaphoreType.DMA((group, SLOTS)),
            pltpu.SemaphoreType.DMA((2,)),
        ],
        compiler_params=pltpu.CompilerParams(vmem_limit_bytes=56 * MIB),
        cost_estimate=SMALL,
        name="attention",
    )(slots, live, queries, output_weight, *tables)


def by_time_kernel(where_ref, piece_ref, *refs):
    refs[-1][0] = piece_ref[...]


def by_time(where, piece, k, step_count, earlier):
    operands, in_specs, aliases = [piece], [pl.BlockSpec(piece.shape, lambda i, w: (0, 0))], {}
    if earlier is not None:
        operands.append(earlier)
        in_specs.append(pl.BlockSpec(memory_space=pl.ANY))
        aliases = {2: 0}
    return pl.pallas_call(
        by_time_kernel,
        grid_spec=pltpu.PrefetchScalarGridSpec(
            num_scalar_prefetch=1,
            grid=(1,),
            in_specs=in_specs,
            out_specs=pl.BlockSpec((1,) + piece.shape, lambda i, w: (w[1] ^ k, 0, 0)),
        ),
        out_shape=jax.ShapeDtypeStruct((step_count,) + piece.shape, piece.dtype),
        input_output_aliases=aliases,
        compiler_params=pltpu.CompilerParams(vmem_limit_bytes=8 * MIB),
        cost_estimate=MEDIUM,
        name="by_time",
    )(where, *operands)


def shards(tokens, input_weight, output_weight, neighbours, degree):
    seg_dev, step_count, model_width = tokens.shape
    heads_here = lax.axis_size("head")
    regions = lax.axis_size("region")
    head_index = lax.axis_index("head")
    region_index = lax.axis_index("region")
    across = heads_here // step_count
    z = head_index // across
    x = head_index % across
    dev_blocks = seg_dev // BLOCK

    def z_move(piece, k):
        return lax.ppermute(
            piece, "head", [(i, i ^ (k * across)) for i in range(heads_here)]
        )

    def x_move(piece, k):
        return lax.ppermute(piece, "head", [(i, i ^ k) for i in range(heads_here)])

    def region_move(piece, k):
        return lax.ppermute(piece, "region", [(i, i ^ k) for i in range(regions)])

    where = jnp.stack([region_index, z, x]).astype(jnp.int32)
    places, slots, live = find_indices(
        where, neighbours, degree, across, dev_blocks, step_count
    )
    weight = sort_weight(input_weight)

    by_step = jnp.transpose(
        tokens.reshape(dev_blocks, CHUNKS, ROWS, step_count, model_width), (3, 1, 0, 2, 4)
    )
    to_send = [
        [lax.dynamic_index_in_dim(by_step[:, part], z ^ k, 0, keepdims=False)
         for k in range(step_count)]
        for part in range(CHUNKS)
    ]
    columns, pieces = {}, {}
    near, far = {}, {}
    tables = {"region": None, "direct": None, "handed": None, "query": None}
    arrived, made = {}, {}
    z_pieces = {0: [z_move(piece, k + 1) for k, piece in enumerate(to_send[0][1:])]}

    def to_partner(first, last):
        return jnp.concatenate(
            [
                jnp.concatenate(
                    [near[part]] + [piece[BORDER:] for piece in far[part]], axis=0
                )
                for part in range(first, last)
            ],
            axis=1,
        )

    def direct(part):
        return ([piece[:BORDER] for piece in far[part]], tables["direct"], part)

    split = CHUNKS // 2
    for turn in range(1, CHUNKS + 2):
        x_part, y_part = turn - 1, turn - 2
        held = {}
        if turn < CHUNKS:
            held["z"] = to_send[turn][1:]
        if x_part < CHUNKS:
            columns[x_part] = jnp.concatenate([to_send[x_part][0]] + z_pieces[x_part], axis=0)
            held["x"] = columns[x_part]
        if y_part >= 0:
            near[y_part], *held["y"] = pick(places, pieces[y_part], regions)
        if turn == CHUNKS:
            held["core"] = to_partner(0, split)
        if turn == 1:
            made["index"] = (places, slots, live)
        if turn == 2:
            made["weight"] = weight
        held, made, arrived = lax.optimization_barrier((held, made, arrived))
        if turn == 1:
            places, slots, live = made["index"]
        weight = made.get("weight", weight)
        tables.update({name: made[name] for name in tables if name in made})
        made = {}
        names, groups = [], []
        if "x" in arrived:
            names.append("region")
            groups.append((pieces[turn - 2], tables["region"], turn - 2))
        if "y" in arrived:
            names.append("direct")
            groups.append(direct(turn - 3))
        if "core" in arrived:
            names.append("handed")
            groups.append(([arrived["core"]], tables["handed"], 0))
        if groups:
            names.append("query")
            results = project(weight, groups, (tables["query"], turn - 2))
            made = dict(zip(names, results))
        arrived = {}
        if "x" in held:
            arrived["x"] = [x_move(held["x"], k) for k in range(1, across)]
            pieces[x_part] = [columns[x_part]] + arrived["x"]
        if "y" in held:
            arrived["y"] = [region_move(piece, 2 * (k + 1)) for k, piece in enumerate(held["y"])]
            far[y_part] = arrived["y"]
        if "core" in held:
            arrived["core"] = region_move(held["core"], 1)
        if "z" in held:
            z_pieces[turn] = [z_move(piece, k + 1) for k, piece in enumerate(held["z"])]
    held = to_partner(split, CHUNKS)
    held, made, arrived = lax.optimization_barrier((held, made, arrived))
    tables.update(made)
    handed = region_move(held, 1)
    tables["direct"], tables["handed"] = project(
        weight, [direct(CHUNKS - 1), ([handed], tables["handed"], 1)]
    )
    queries = tables.pop("query")
    tables = [tables["region"], tables["direct"], tables["handed"]]

    back = [None] * step_count
    for k in reversed(range(step_count)):
        result = attention(
            k * dev_blocks, dev_blocks, slots, live, queries, output_weight, tables
        )
        result = result.reshape(seg_dev, model_width)
        back[k] = z_move(result, k) if k else result
    stacked = None
    for k in [0] + list(reversed(range(1, step_count))):
        stacked = by_time(where, back[k], k, step_count, stacked)
    return jnp.transpose(stacked, (1, 0, 2))


def solution(mesh):
    in_specs = (P(("region", "head"), None, None), P(), P(), P(), P())
    out_specs = P(("region", "head"), None, None)
    return jax.shard_map(shards, mesh=mesh, in_specs=in_specs, out_specs=out_specs, check_vma=False)
```

```python
import functools
import math

import jax
import jax.numpy as jnp
from jax import lax
from jax.experimental import pallas as pl
from jax.experimental.pallas import tpu as pltpu
from jax.sharding import PartitionSpec as P

HEADS = 16
HEAD_SIZE = 64
BLOCK = 128
SLOTS = 8
BORDER = 4
CHUNKS = 4
ROWS = BLOCK // CHUNKS
PAIR = 2 * HEAD_SIZE
UNROLL = 4
TILE = 512
MIB = 1024 * 1024
RESIDENT = 20 * MIB
PROJECT_LIMIT = 24 * MIB
ATTENTION_LIMIT = 24 * MIB
LOG2E = math.log2(math.e)
MEDIUM = pl.CostEstimate(flops=15 * 10**7, bytes_accessed=5 * 10**5, transcendentals=0)
SMALL = pl.CostEstimate(flops=1000, bytes_accessed=1000, transcendentals=0)

VMEM = pl.BlockSpec(memory_space=pltpu.VMEM)
SMEM = pl.BlockSpec(memory_space=pltpu.SMEM)
ANYWHERE = pl.BlockSpec(memory_space=pl.ANY)


def weight_kernel(in_ref, out_ref):
    rows, columns = out_ref.shape
    width = columns // 3
    low = lax.broadcasted_iota(jnp.int32, (rows, PAIR), 1) < HEAD_SIZE
    for pair in range(width // PAIR):
        one = in_ref[:, 3 * pair * PAIR : (3 * pair + 1) * PAIR]
        two = in_ref[:, (3 * pair + 1) * PAIR : (3 * pair + 2) * PAIR]
        three = in_ref[:, (3 * pair + 2) * PAIR : (3 * pair + 3) * PAIR]
        keys = jnp.concatenate([one[:, HEAD_SIZE:], three[:, :HEAD_SIZE]], axis=1)
        for number, value in enumerate(
            (keys, jnp.where(low, two, three), jnp.where(low, one, two))
        ):
            first = number * width + pair * PAIR
            out_ref[:, first : first + PAIR] = value


def sort_weight(weight):
    depth, columns = weight.shape
    rows = 128
    return pl.pallas_call(
        weight_kernel,
        grid=(depth // rows,),
        out_shape=jax.ShapeDtypeStruct((depth, columns), weight.dtype),
        in_specs=[pl.BlockSpec((rows, columns), lambda i: (i, 0))],
        out_specs=pl.BlockSpec((rows, columns), lambda i: (i, 0)),
        compiler_params=pltpu.CompilerParams(vmem_limit_bytes=8 * MIB),
        cost_estimate=SMALL,
        name="sort_weight",
    )(weight)


def index_kernel(
    across, dev_blocks, step_count, where_ref, list_ref, degree_ref,
    place_ref, slot_ref, live_ref, mark_ref, rank_ref,
):
    region, z, x = where_ref[0], where_ref[1], where_ref[2]
    blocks = list_ref.shape[0]
    region_blocks = across * dev_blocks * step_count
    column_blocks = dev_blocks * step_count
    regions = blocks // region_blocks

    def home(local):
        owner = local // dev_blocks
        return (
            ((owner % across) ^ x) * column_blocks
            + ((owner // across) ^ z) * dev_blocks
            + local % dev_blocks
        )

    def clear(i, carry):
        mark_ref[i] = 0
        rank_ref[i] = 0
        return carry

    lax.fori_loop(0, blocks, clear, 0)

    def look(block, carry):
        namer = block // region_blocks
        for slot in range(SLOTS):
            name = list_ref[block, slot]
            named_region = name // region_blocks

            @pl.when(named_region == region)
            def _():
                mark_ref[namer * region_blocks + name % region_blocks] = 1

            @pl.when(namer == region)
            def _():
                rank_ref[name] = 1

        return carry

    lax.fori_loop(0, blocks, look, 0)

    def clear_places(i, carry):
        place_ref[i] = 0
        return carry

    lax.fori_loop(0, (regions - 1) * BORDER, clear_places, 0)

    def ranks(k, carry):
        other = region ^ k

        def one(local, counts):
            sent, got = counts
            marked = mark_ref[other * region_blocks + local]

            @pl.when((marked == 1) & (sent < BORDER))
            def _():
                place_ref[(k - 1) * BORDER + jnp.minimum(sent, BORDER - 1)] = home(local)

            named = rank_ref[other * region_blocks + local]
            rank_ref[other * region_blocks + local] = got
            return sent + marked, got + named

        lax.fori_loop(0, region_blocks, one, (0, 0))
        return carry

    lax.fori_loop(1, regions, ranks, 0)

    def lists(i, carry):
        local = (((i // dev_blocks) ^ z) * across + x) * dev_blocks + i % dev_blocks
        block = region * region_blocks + local
        live_ref[i] = degree_ref[block]
        for slot in range(SLOTS):
            name = list_ref[block, slot]
            source = (name // region_blocks) ^ region
            direct = (source // 2 - 1) * BORDER
            handed = (regions // 2 - 1 + source // 2) * BORDER
            remote = region_blocks + jnp.where(source % 2 == 0, direct, handed) + rank_ref[name]
            slot_ref[i, slot] = jnp.where(source == 0, home(name % region_blocks), remote)
        return carry

    lax.fori_loop(0, column_blocks, lists, 0)


def find_indices(where, neighbours, degree, across, dev_blocks, step_count):
    blocks = neighbours.shape[0]
    region_blocks = across * dev_blocks * step_count
    regions = blocks // region_blocks
    column_blocks = dev_blocks * step_count
    return pl.pallas_call(
        functools.partial(index_kernel, across, dev_blocks, step_count),
        out_shape=[
            jax.ShapeDtypeStruct(((regions - 1) * BORDER,), jnp.int32),
            jax.ShapeDtypeStruct((column_blocks, SLOTS), jnp.int32),
            jax.ShapeDtypeStruct((column_blocks,), jnp.int32),
        ],
        in_specs=[SMEM] * 3,
        out_specs=[SMEM] * 3,
        scratch_shapes=[pltpu.SMEM((blocks,), jnp.int32), pltpu.SMEM((blocks,), jnp.int32)],
        compiler_params=pltpu.CompilerParams(vmem_limit_bytes=1 * MIB),
        cost_estimate=SMALL,
        name="find_indices",
    )(where, neighbours, degree)


def project_kernel(groups, query, counts, *refs):
    total = sum(counts)
    weight_ref = refs[total]
    *outs, flat, stage, sems = refs
    if query is not None:
        *outs, q_ref = outs
    table_ref = outs[-1]
    width = table_ref.shape[2] // 2

    first = 0
    for piece in refs[:total]:
        rows = piece.shape[0] * piece.shape[1]
        flat[first : first + rows] = piece[...].reshape(rows, piece.shape[2])
        first += rows

    tiles = []
    for tile in range(0, 2 * width, TILE):
        targets = []
        first = 0
        for blocks, rows, first_block, first_row in groups:
            targets.append((first, blocks, rows, table_ref, first_block, first_row, tile))
            first += blocks * rows
        tiles.append((tile, first, targets))
    if query is not None:
        blocks, rows, first_row = query
        for tile in range(0, width, TILE):
            targets = [(0, blocks, rows, q_ref, 0, first_row, tile)]
            tiles.append((2 * width + tile, blocks * rows, targets))

    waiting = {0: [], 1: []}
    for number, (column, height, targets) in enumerate(tiles):
        slot = number % 2
        result = jnp.dot(
            flat[:height], weight_ref[:, column : column + TILE],
            preferred_element_type=jnp.float32,
        ).astype(jnp.bfloat16)
        for copy in waiting[slot]:
            copy.wait()
        waiting[slot] = []
        stage[slot, :height] = result
        for index, (first, blocks, rows, out_ref, first_block, first_row, tile) in enumerate(
            targets
        ):
            copy = pltpu.make_async_copy(
                stage.at[slot, pl.ds(first, blocks * rows), :].reshape(blocks, rows, TILE),
                out_ref.at[
                    pl.ds(first_block, blocks), pl.ds(first_row, rows), pl.ds(tile, TILE)
                ],
                sems.at[slot, index],
            )
            copy.start()
            waiting[slot].append(copy)
    for copies in waiting.values():
        for copy in copies:
            copy.wait()


def project(weight, groups, table, table_blocks, queries=None, query_row=None):
    depth, columns = weight.shape
    width = columns // 3
    operands, counts, shapes = [], [], []
    all_rows = 0
    for pieces, first_block, first_row in groups:
        blocks = sum(piece.shape[0] for piece in pieces)
        rows = pieces[0].shape[1]
        operands += pieces
        counts.append(len(pieces))
        shapes.append((blocks, rows, first_block, first_row))
        all_rows += blocks * rows
    operands.append(weight)
    in_specs = [VMEM] * len(operands)
    old = [table]
    out_shape = [jax.ShapeDtypeStruct((table_blocks, BLOCK, 2 * width), jnp.bfloat16)]
    query = None
    if query_row is not None:
        blocks, rows = groups[0][0][0].shape[:2]
        query = (blocks, rows, query_row)
        old.append(queries)
        out_shape.append(jax.ShapeDtypeStruct((blocks, BLOCK, width), jnp.bfloat16))
    aliases = {}
    for number, array in enumerate(old):
        if array is not None:
            aliases[len(operands)] = number
            operands.append(array)
            in_specs.append(ANYWHERE)
    return pl.pallas_call(
        functools.partial(project_kernel, tuple(shapes), query, tuple(counts)),
        out_shape=out_shape,
        in_specs=in_specs,
        out_specs=[ANYWHERE] * len(out_shape),
        scratch_shapes=[
            pltpu.VMEM((all_rows, depth), jnp.bfloat16),
            pltpu.VMEM((2, all_rows, TILE), jnp.bfloat16),
            pltpu.SemaphoreType.DMA((2, len(groups))),
        ],
        input_output_aliases=aliases,
        compiler_params=pltpu.CompilerParams(vmem_limit_bytes=PROJECT_LIMIT),
        cost_estimate=SMALL,
        name="project",
    )(*operands)


def pick_kernel(count, place_ref, *refs):
    pieces = refs[:count]
    part_blocks = pieces[0].shape[0]
    item = 0
    for out_ref in refs[count:]:
        for here in range(out_ref.shape[0]):
            place = place_ref[item]
            item += 1
            for index, piece in enumerate(pieces):

                @pl.when(place // part_blocks == index)
                def _():
                    out_ref[here] = piece[place % part_blocks]


def pick(places, pieces, counts):
    return pl.pallas_call(
        functools.partial(pick_kernel, len(pieces)),
        out_shape=[
            jax.ShapeDtypeStruct((count,) + pieces[0].shape[1:], pieces[0].dtype)
            for count in counts
        ],
        in_specs=[SMEM] + [VMEM] * len(pieces),
        out_specs=[VMEM] * len(counts),
        compiler_params=pltpu.CompilerParams(vmem_limit_bytes=8 * MIB),
        cost_estimate=SMALL,
        name="pick",
    )(places, *pieces)


def attend_block(slots, last_bias, width, load_q, load_kv, store):
    first = lax.broadcasted_iota(jnp.int32, (BLOCK, PAIR), 1) < HEAD_SIZE

    def one_pair(pair):
        columns = pl.ds(pl.multiple_of(pair * PAIR, PAIR), PAIR)
        values_at = pl.ds(pl.multiple_of(width + pair * PAIR, PAIR), PAIR)
        q = load_q(columns)
        zero = jnp.zeros_like(q)
        q_two = jnp.concatenate([jnp.where(first, q, zero), jnp.where(first, zero, q)], axis=0)
        keys = jnp.concatenate([load_kv(slot, columns) for slot in range(slots)], axis=0)
        values = jnp.concatenate([load_kv(slot, values_at) for slot in range(slots)], axis=0)
        scores = lax.dot_general(
            q_two, keys, (((1,), (1,)), ((), ())), preferred_element_type=jnp.float32
        )
        scores = jnp.concatenate([scores[:, :-BLOCK], scores[:, -BLOCK:] + last_bias], axis=1)
        top = jnp.max(scores, axis=1, keepdims=True)
        exponent = jnp.exp2((scores - top) * (HEAD_SIZE ** (-0.5) * LOG2E))
        total = jnp.sum(exponent, axis=1, keepdims=True)
        mixed = jnp.dot(
            exponent.astype(jnp.bfloat16), values, preferred_element_type=jnp.float32
        )
        mixed = mixed / total
        store(columns, jnp.where(first, mixed[:BLOCK], mixed[BLOCK:]).astype(jnp.bfloat16))

    def some_pairs(i, carry):
        for u in range(UNROLL):
            one_pair(i * UNROLL + u)
        return carry

    lax.fori_loop(0, width // PAIR // UNROLL, some_pairs, 0)


def attention_kernel(resident, start_ref, slot_ref, live_ref, q_ref, w_ref, table, out_ref, *scratch):
    group, _, width = out_ref.shape
    start = start_ref[0]
    att_buf = scratch[0]

    def place(block, slot):
        return slot_ref[block, jnp.where(slot < live_ref[block], slot, 0)]

    if not resident:
        kv_buf, sems = scratch[1:]

        def copies(block, action):
            def one(slot, carry):
                copy = pltpu.make_async_copy(
                    table.at[place(start + block, slot)], kv_buf.at[block, slot],
                    sems.at[block, slot],
                )
                if action == "start":
                    copy.start()
                else:
                    copy.wait()
                return carry

            lax.fori_loop(0, (live_ref[start + block] + 1) // 2 * 2, one, 0)

        for block in range(group):
            copies(block, "start")

    def one_block(block, carry):
        live = live_ref[start + block]
        if not resident:
            copies(block, "wait")

        def load_q(columns):
            return q_ref[start + block, :, columns]

        def load_kv(slot, columns):
            if resident:
                return table[place(start + block, slot), :, columns]
            return kv_buf[block, slot, :, columns]

        def store(columns, value):
            att_buf[block, :, columns] = value

        last_bias = jnp.where(live % 2 == 1, -jnp.inf, 0.0).astype(jnp.float32)
        for slots in range(2, SLOTS + 1, 2):

            @pl.when((live + 1) // 2 * 2 == slots)
            def _():
                attend_block(slots, last_bias, width, load_q, load_kv, store)

        return carry

    lax.fori_loop(0, group, one_block, 0)
    flat = att_buf[...].reshape(group * BLOCK, width)

    def one_tile(tile, carry):
        here = pl.ds(pl.multiple_of(tile * TILE, TILE), TILE)
        out_ref[:, :, here] = (
            jnp.dot(flat, w_ref[:, here], preferred_element_type=jnp.float32)
            .astype(jnp.bfloat16)
            .reshape(group, BLOCK, TILE)
        )
        return carry

    lax.fori_loop(0, width // TILE, one_tile, 0)


def attention(start, group, slots, live, queries, output_weight, table):
    width = queries.shape[2]
    resident = is_resident(table.shape)
    scratch = [pltpu.VMEM((group, BLOCK, width), jnp.bfloat16)]
    if not resident:
        scratch += [
            pltpu.VMEM((group, SLOTS, BLOCK, 2 * width), jnp.bfloat16),
            pltpu.SemaphoreType.DMA((group, SLOTS)),
        ]
    return pl.pallas_call(
        functools.partial(attention_kernel, resident),
        out_shape=jax.ShapeDtypeStruct((group, BLOCK, width), jnp.bfloat16),
        in_specs=[SMEM, SMEM, SMEM, VMEM, VMEM, VMEM if resident else ANYWHERE],
        out_specs=VMEM,
        scratch_shapes=scratch,
        compiler_params=pltpu.CompilerParams(vmem_limit_bytes=ATTENTION_LIMIT),
        cost_estimate=SMALL,
        name="attention",
    )(jnp.full((1,), start, jnp.int32), slots, live, queries, output_weight, table)


def is_resident(shape):
    return 2 * math.prod(shape) <= RESIDENT


def by_time_kernel(where_ref, piece_ref, *refs):
    refs[-1][0] = piece_ref[...]


def by_time(where, piece, k, part, shape, earlier):
    operands, in_specs, aliases = [piece], [pl.BlockSpec(piece.shape, lambda i, w: (0, 0))], {}
    if earlier is not None:
        operands.append(earlier)
        in_specs.append(pl.BlockSpec(memory_space=pl.ANY))
        aliases = {2: 0}
    return pl.pallas_call(
        by_time_kernel,
        grid_spec=pltpu.PrefetchScalarGridSpec(
            num_scalar_prefetch=1,
            grid=(1,),
            in_specs=in_specs,
            out_specs=pl.BlockSpec((1,) + piece.shape, lambda i, w: (w[1] ^ k, part, 0)),
        ),
        out_shape=jax.ShapeDtypeStruct(shape, piece.dtype),
        input_output_aliases=aliases,
        compiler_params=pltpu.CompilerParams(vmem_limit_bytes=8 * MIB),
        cost_estimate=MEDIUM,
        name="by_time",
    )(where, *operands)


def shards(tokens, input_weight, output_weight, neighbours, degree):
    seg_dev, step_count, model_width = tokens.shape
    heads_here = lax.axis_size("head")
    regions = lax.axis_size("region")
    head_index = lax.axis_index("head")
    region_index = lax.axis_index("region")
    across = heads_here // step_count
    z = head_index // across
    x = head_index % across
    dev_blocks = seg_dev // BLOCK

    def z_move(piece, k):
        return lax.ppermute(
            piece, "head", [(i, i ^ (k * across)) for i in range(heads_here)]
        )

    def x_move(piece, k):
        return lax.ppermute(piece, "head", [(i, i ^ k) for i in range(heads_here)])

    def region_move(piece, k):
        return lax.ppermute(piece, "region", [(i, i ^ k) for i in range(regions)])

    where = jnp.stack([region_index, z, x]).astype(jnp.int32)
    places, slots, live = find_indices(
        where, neighbours, degree, across, dev_blocks, step_count
    )
    weight = sort_weight(input_weight)

    by_step = jnp.transpose(
        tokens.reshape(dev_blocks, CHUNKS, ROWS, step_count, model_width), (3, 1, 0, 2, 4)
    )
    to_send = [
        [lax.dynamic_index_in_dim(by_step[:, part], z ^ k, 0, keepdims=False)
         for k in range(step_count)]
        for part in range(CHUNKS)
    ]
    columns, pieces = {}, {}
    near, far = {}, {}
    region_blocks = dev_blocks * heads_here
    direct_first = region_blocks
    handed_first = region_blocks + (regions // 2 - 1) * BORDER
    table_blocks = region_blocks + (regions - 1) * BORDER
    split = CHUNKS // 2
    table, queries = None, None
    arrived, made = {}, {}
    z_pieces = {0: [z_move(piece, k + 1) for k, piece in enumerate(to_send[0][1:])]}

    def border_groups(part):
        row = part * ROWS
        if part < split:
            return [([piece[:BORDER] for piece in far[part]], direct_first, row)]
        by_region = [near[part]] + far[part]
        return [
            (by_region[1::2], direct_first, row),
            (by_region[0::2], handed_first, row),
        ]

    for turn in range(1, CHUNKS + 2):
        x_part, y_part = turn - 1, turn - 2
        held = {}
        if turn < CHUNKS:
            held["z"] = to_send[turn][1:]
        if x_part < CHUNKS:
            columns[x_part] = jnp.concatenate([to_send[x_part][0]] + z_pieces[x_part], axis=0)
            held["x"] = columns[x_part]
        if 0 <= y_part < split:
            near[y_part], *held["y"] = pick(
                places, pieces[y_part], [BORDER] + [2 * BORDER] * (regions // 2 - 1)
            )
        elif y_part >= split:
            held["y"] = pick(places, pieces[y_part], [BORDER] * (regions - 1))
        if turn == CHUNKS:
            held["core"] = jnp.concatenate(
                [
                    jnp.concatenate(
                        [near[part]] + [piece[BORDER:] for piece in far[part]], axis=0
                    )
                    for part in range(split)
                ],
                axis=1,
            )
        if turn == 1:
            made["index"] = (places, slots, live)
        if turn == 2:
            made["weight"] = weight
        held, made, arrived = lax.optimization_barrier((held, made, arrived))
        if turn == 1:
            places, slots, live = made["index"]
        weight = made.get("weight", weight)
        table, queries = made.get("table", (table, queries))
        made = {}
        groups = []
        if "x" in arrived:
            groups.append((pieces[turn - 2], 0, (turn - 2) * ROWS))
        if "y" in arrived:
            groups += border_groups(turn - 3)
        if "core" in arrived:
            groups.append(([arrived["core"]], handed_first, 0))
        if groups:
            made["table"] = project(
                weight, groups, table, table_blocks, queries, (turn - 2) * ROWS
            )
        arrived = {}
        if "x" in held:
            arrived["x"] = [x_move(held["x"], k) for k in range(1, across)]
            pieces[x_part] = [columns[x_part]] + arrived["x"]
        if "y" in held:
            if y_part < split:
                moved = [region_move(piece, 2 * (k + 1)) for k, piece in enumerate(held["y"])]
                far[y_part] = moved
            else:
                moved = [region_move(piece, k + 1) for k, piece in enumerate(held["y"])]
                near[y_part], *far[y_part] = moved
            arrived["y"] = moved
        if "core" in held:
            arrived["core"] = region_move(held["core"], 1)
        if "z" in held:
            z_pieces[turn] = [z_move(piece, k + 1) for k, piece in enumerate(held["z"])]
    table, queries = made["table"]
    (table,) = project(weight, border_groups(CHUNKS - 1), table, table_blocks)

    calls = [(k, block, 1) for k in reversed(range(step_count)) for block in range(dev_blocks)]
    results = {}
    for k, block, count in calls:
        result = attention(
            k * dev_blocks + block, count, slots, live, queries, output_weight, table
        )
        slots, result = lax.optimization_barrier((slots, result))
        result = result.reshape(count * BLOCK, model_width)
        results[k, block, count] = z_move(result, k) if k else result
    stacked = None
    for k, block, count in calls[-dev_blocks:] + calls[:-dev_blocks]:
        stacked = by_time(
            where, results[k, block, count], k, block // count,
            (step_count, seg_dev, model_width), stacked,
        )
    return jnp.transpose(stacked, (1, 0, 2))


def solution(mesh):
    in_specs = (P(("region", "head"), None, None), P(), P(), P(), P())
    out_specs = P(("region", "head"), None, None)
    return jax.shard_map(shards, mesh=mesh, in_specs=in_specs, out_specs=out_specs, check_vma=False)
```

```python
import functools
import math

import jax
import jax.numpy as jnp
from jax import lax
from jax.experimental import pallas as pl
from jax.experimental.pallas import tpu as pltpu
from jax.sharding import PartitionSpec as P

HEADS = 16
HEAD_SIZE = 64
BLOCK = 128
SLOTS = 8
BORDER = 4
CHUNKS = 4
ROWS = BLOCK // CHUNKS
PAIR = 2 * HEAD_SIZE
UNROLL = 4
TILE = 512
MIB = 1024 * 1024
RESIDENT = 20 * MIB
PROJECT_LIMIT = 24 * MIB
ATTENTION_LIMIT = 24 * MIB
LOG2E = math.log2(math.e)
MEDIUM = pl.CostEstimate(flops=15 * 10**7, bytes_accessed=5 * 10**5, transcendentals=0)
SMALL = pl.CostEstimate(flops=1000, bytes_accessed=1000, transcendentals=0)

VMEM = pl.BlockSpec(memory_space=pltpu.VMEM)
SMEM = pl.BlockSpec(memory_space=pltpu.SMEM)
ANYWHERE = pl.BlockSpec(memory_space=pl.ANY)


def weight_kernel(in_ref, out_ref):
    rows, columns = out_ref.shape
    width = columns // 3
    low = lax.broadcasted_iota(jnp.int32, (rows, PAIR), 1) < HEAD_SIZE
    for pair in range(width // PAIR):
        one = in_ref[:, 3 * pair * PAIR : (3 * pair + 1) * PAIR]
        two = in_ref[:, (3 * pair + 1) * PAIR : (3 * pair + 2) * PAIR]
        three = in_ref[:, (3 * pair + 2) * PAIR : (3 * pair + 3) * PAIR]
        keys = jnp.concatenate([one[:, HEAD_SIZE:], three[:, :HEAD_SIZE]], axis=1)
        for number, value in enumerate(
            (keys, jnp.where(low, two, three), jnp.where(low, one, two))
        ):
            first = number * width + pair * PAIR
            out_ref[:, first : first + PAIR] = value


def sort_weight(weight):
    depth, columns = weight.shape
    rows = 128
    return pl.pallas_call(
        weight_kernel,
        grid=(depth // rows,),
        out_shape=jax.ShapeDtypeStruct((depth, columns), weight.dtype),
        in_specs=[pl.BlockSpec((rows, columns), lambda i: (i, 0))],
        out_specs=pl.BlockSpec((rows, columns), lambda i: (i, 0)),
        compiler_params=pltpu.CompilerParams(vmem_limit_bytes=8 * MIB),
        cost_estimate=SMALL,
        name="sort_weight",
    )(weight)


def index_kernel(
    across, dev_blocks, step_count, where_ref, list_ref, degree_ref,
    place_ref, slot_ref, live_ref, mark_ref, rank_ref,
):
    region, z, x = where_ref[0], where_ref[1], where_ref[2]
    blocks = list_ref.shape[0]
    region_blocks = across * dev_blocks * step_count
    column_blocks = dev_blocks * step_count
    regions = blocks // region_blocks

    def split(number, size):
        high = lax.div(number, jnp.int32(size))
        return high, number - high * size

    def home(local):
        owner, block = split(local, dev_blocks)
        owner_z, owner_x = split(owner, across)
        return (owner_x ^ x) * column_blocks + (owner_z ^ z) * dev_blocks + block

    def clear(i, carry):
        mark_ref[i] = 0
        rank_ref[i] = 0
        return carry

    lax.fori_loop(0, blocks, clear, 0, unroll=8)
    ours = region * region_blocks

    def look_from(namer, carry):
        base = namer * region_blocks

        def look(i, c):
            for slot in range(SLOTS):
                local = list_ref[base + i, slot] - ours
                inside = (local >= 0) & (local < region_blocks)
                mark_ref[jnp.where(inside, base + local, blocks)] = 1
            return c

        lax.fori_loop(0, region_blocks, look, 0)
        return carry

    lax.fori_loop(0, regions, look_from, 0)

    def look_here(i, carry):
        for slot in range(SLOTS):
            rank_ref[list_ref[ours + i, slot]] = 1
        return carry

    lax.fori_loop(0, region_blocks, look_here, 0)

    unused = (regions - 1) * BORDER

    def clear_places(i, carry):
        place_ref[i] = 0
        return carry

    lax.fori_loop(0, unused, clear_places, 0)

    def ranks(k, carry):
        base = (region ^ k) * region_blocks

        def one(local, counts):
            sent, got = counts
            marked = mark_ref[base + local]
            use = (marked == 1) & (sent < BORDER)
            place_ref[jnp.where(use, (k - 1) * BORDER + sent, unused)] = home(local)
            named = rank_ref[base + local]
            rank_ref[base + local] = got
            return sent + marked, got + named

        lax.fori_loop(0, region_blocks, one, (0, 0))
        return carry

    lax.fori_loop(1, regions, ranks, 0)

    def lists(i, carry):
        distance, block = split(i, dev_blocks)
        local = ((distance ^ z) * across + x) * dev_blocks + block
        live_ref[i] = degree_ref[ours + local]
        for slot in range(SLOTS):
            name = list_ref[ours + local, slot]
            name_region, name_local = split(name, region_blocks)
            source = name_region ^ region
            direct = ((source >> 1) - 1) * BORDER
            handed = (regions // 2 - 1 + (source >> 1)) * BORDER
            remote = region_blocks + jnp.where((source & 1) == 0, direct, handed) + rank_ref[name]
            slot_ref[i, slot] = jnp.where(source == 0, home(name_local), remote)
        return carry

    lax.fori_loop(0, column_blocks, lists, 0)


def find_indices(where, neighbours, degree, across, dev_blocks, step_count):
    blocks = neighbours.shape[0]
    region_blocks = across * dev_blocks * step_count
    regions = blocks // region_blocks
    column_blocks = dev_blocks * step_count
    return pl.pallas_call(
        functools.partial(index_kernel, across, dev_blocks, step_count),
        out_shape=[
            jax.ShapeDtypeStruct(((regions - 1) * BORDER + 1,), jnp.int32),
            jax.ShapeDtypeStruct((column_blocks, SLOTS), jnp.int32),
            jax.ShapeDtypeStruct((column_blocks,), jnp.int32),
        ],
        in_specs=[SMEM] * 3,
        out_specs=[SMEM] * 3,
        scratch_shapes=[pltpu.SMEM((blocks + 1,), jnp.int32), pltpu.SMEM((blocks + 1,), jnp.int32)],
        compiler_params=pltpu.CompilerParams(vmem_limit_bytes=1 * MIB),
        cost_estimate=SMALL,
        name="find_indices",
    )(where, neighbours, degree)


def project_kernel(groups, query, counts, *refs):
    total = sum(counts)
    weight_ref = refs[total]
    *outs, flat, stage, sems = refs
    if query is not None:
        *outs, q_ref = outs
    table_ref = outs[-1]
    width = table_ref.shape[2] // 2

    first = 0
    for piece in refs[:total]:
        rows = piece.shape[0] * piece.shape[1]
        flat[first : first + rows] = piece[...].reshape(rows, piece.shape[2])
        first += rows

    tiles = []
    for tile in range(0, 2 * width, TILE):
        targets = []
        first = 0
        for blocks, rows, first_block, first_row in groups:
            targets.append((first, blocks, rows, table_ref, first_block, first_row, tile))
            first += blocks * rows
        tiles.append((tile, first, targets))
    if query is not None:
        blocks, rows, first_row = query
        for tile in range(0, width, TILE):
            targets = [(0, blocks, rows, q_ref, 0, first_row, tile)]
            tiles.append((2 * width + tile, blocks * rows, targets))

    waiting = {0: [], 1: []}
    for number, (column, height, targets) in enumerate(tiles):
        slot = number % 2
        result = jnp.dot(
            flat[:height], weight_ref[:, column : column + TILE],
            preferred_element_type=jnp.float32,
        ).astype(jnp.bfloat16)
        for copy in waiting[slot]:
            copy.wait()
        waiting[slot] = []
        stage[slot, :height] = result
        for index, (first, blocks, rows, out_ref, first_block, first_row, tile) in enumerate(
            targets
        ):
            copy = pltpu.make_async_copy(
                stage.at[slot, pl.ds(first, blocks * rows), :].reshape(blocks, rows, TILE),
                out_ref.at[
                    pl.ds(first_block, blocks), pl.ds(first_row, rows), pl.ds(tile, TILE)
                ],
                sems.at[slot, index],
            )
            copy.start()
            waiting[slot].append(copy)
    for copies in waiting.values():
        for copy in copies:
            copy.wait()


def project(weight, groups, table, table_blocks, queries=None, query_row=None):
    depth, columns = weight.shape
    width = columns // 3
    operands, counts, shapes = [], [], []
    all_rows = 0
    for pieces, first_block, first_row in groups:
        blocks = sum(piece.shape[0] for piece in pieces)
        rows = pieces[0].shape[1]
        operands += pieces
        counts.append(len(pieces))
        shapes.append((blocks, rows, first_block, first_row))
        all_rows += blocks * rows
    operands.append(weight)
    in_specs = [VMEM] * len(operands)
    old = [table]
    out_shape = [jax.ShapeDtypeStruct((table_blocks, BLOCK, 2 * width), jnp.bfloat16)]
    query = None
    if query_row is not None:
        blocks, rows = groups[0][0][0].shape[:2]
        query = (blocks, rows, query_row)
        old.append(queries)
        out_shape.append(jax.ShapeDtypeStruct((blocks, BLOCK, width), jnp.bfloat16))
    aliases = {}
    for number, array in enumerate(old):
        if array is not None:
            aliases[len(operands)] = number
            operands.append(array)
            in_specs.append(ANYWHERE)
    return pl.pallas_call(
        functools.partial(project_kernel, tuple(shapes), query, tuple(counts)),
        out_shape=out_shape,
        in_specs=in_specs,
        out_specs=[ANYWHERE] * len(out_shape),
        scratch_shapes=[
            pltpu.VMEM((all_rows, depth), jnp.bfloat16),
            pltpu.VMEM((2, all_rows, TILE), jnp.bfloat16),
            pltpu.SemaphoreType.DMA((2, len(groups))),
        ],
        input_output_aliases=aliases,
        compiler_params=pltpu.CompilerParams(vmem_limit_bytes=PROJECT_LIMIT),
        cost_estimate=pl.CostEstimate(
            flops=4 * all_rows * depth * width, bytes_accessed=6 * all_rows * depth,
            transcendentals=0,
        ),
        name="project",
    )(*operands)


def pick_kernel(count, place_ref, *refs):
    pieces = refs[:count]
    part_blocks = pieces[0].shape[0]
    item = 0
    for out_ref in refs[count:]:
        for here in range(out_ref.shape[0]):
            place = place_ref[item]
            item += 1
            for index, piece in enumerate(pieces):

                @pl.when(place // part_blocks == index)
                def _():
                    out_ref[here] = piece[place % part_blocks]


def pick(places, pieces, counts):
    return pl.pallas_call(
        functools.partial(pick_kernel, len(pieces)),
        out_shape=[
            jax.ShapeDtypeStruct((count,) + pieces[0].shape[1:], pieces[0].dtype)
            for count in counts
        ],
        in_specs=[SMEM] + [VMEM] * len(pieces),
        out_specs=[VMEM] * len(counts),
        compiler_params=pltpu.CompilerParams(vmem_limit_bytes=8 * MIB),
        cost_estimate=SMALL,
        name="pick",
    )(places, *pieces)


def attend_block(slots, last_bias, width, load_q, load_kv, store):
    first = lax.broadcasted_iota(jnp.int32, (BLOCK, PAIR), 1) < HEAD_SIZE

    def one_pair(pair):
        columns = pl.ds(pl.multiple_of(pair * PAIR, PAIR), PAIR)
        values_at = pl.ds(pl.multiple_of(width + pair * PAIR, PAIR), PAIR)
        q = load_q(columns)
        zero = jnp.zeros_like(q)
        q_two = jnp.concatenate([jnp.where(first, q, zero), jnp.where(first, zero, q)], axis=0)
        keys = jnp.concatenate([load_kv(slot, columns) for slot in range(slots)], axis=0)
        values = jnp.concatenate([load_kv(slot, values_at) for slot in range(slots)], axis=0)
        scores = lax.dot_general(
            q_two, keys, (((1,), (1,)), ((), ())), preferred_element_type=jnp.float32
        )
        scores = jnp.concatenate([scores[:, :-BLOCK], scores[:, -BLOCK:] + last_bias], axis=1)
        top = jnp.max(scores, axis=1, keepdims=True)
        exponent = jnp.exp2((scores - top) * (HEAD_SIZE ** (-0.5) * LOG2E))
        total = jnp.sum(exponent, axis=1, keepdims=True)
        mixed = jnp.dot(
            exponent.astype(jnp.bfloat16), values, preferred_element_type=jnp.float32
        )
        mixed = mixed / total
        store(columns, jnp.where(first, mixed[:BLOCK], mixed[BLOCK:]).astype(jnp.bfloat16))

    def some_pairs(i, carry):
        for u in range(UNROLL):
            one_pair(i * UNROLL + u)
        return carry

    lax.fori_loop(0, width // PAIR // UNROLL, some_pairs, 0)


def attention_kernel(resident, start_ref, slot_ref, live_ref, q_ref, w_ref, table, out_ref, *scratch):
    group, _, width = out_ref.shape
    start = start_ref[0]
    att_buf = scratch[0]

    def place(block, slot):
        return slot_ref[block, jnp.where(slot < live_ref[block], slot, 0)]

    if not resident:
        kv_buf, sems = scratch[1:]

        def copies(block, action):
            def one(slot, carry):
                copy = pltpu.make_async_copy(
                    table.at[place(start + block, slot)], kv_buf.at[block, slot],
                    sems.at[block, slot],
                )
                if action == "start":
                    copy.start()
                else:
                    copy.wait()
                return carry

            lax.fori_loop(0, (live_ref[start + block] + 1) // 2 * 2, one, 0)

        for block in range(group):
            copies(block, "start")

    def one_block(block, carry):
        live = live_ref[start + block]
        if not resident:
            copies(block, "wait")

        def load_q(columns):
            return q_ref[start + block, :, columns]

        def load_kv(slot, columns):
            if resident:
                return table[place(start + block, slot), :, columns]
            return kv_buf[block, slot, :, columns]

        def store(columns, value):
            att_buf[block, :, columns] = value

        last_bias = jnp.where(live % 2 == 1, -jnp.inf, 0.0).astype(jnp.float32)
        for slots in range(2, SLOTS + 1, 2):

            @pl.when((live + 1) // 2 * 2 == slots)
            def _():
                attend_block(slots, last_bias, width, load_q, load_kv, store)

        return carry

    lax.fori_loop(0, group, one_block, 0)
    flat = att_buf[...].reshape(group * BLOCK, width)

    def one_tile(tile, carry):
        here = pl.ds(pl.multiple_of(tile * TILE, TILE), TILE)
        out_ref[:, :, here] = (
            jnp.dot(flat, w_ref[:, here], preferred_element_type=jnp.float32)
            .astype(jnp.bfloat16)
            .reshape(group, BLOCK, TILE)
        )
        return carry

    lax.fori_loop(0, width // TILE, one_tile, 0)


def attention(start, group, slots, live, queries, output_weight, table):
    width = queries.shape[2]
    resident = is_resident(table.shape)
    scratch = [pltpu.VMEM((group, BLOCK, width), jnp.bfloat16)]
    if not resident:
        scratch += [
            pltpu.VMEM((group, SLOTS, BLOCK, 2 * width), jnp.bfloat16),
            pltpu.SemaphoreType.DMA((group, SLOTS)),
        ]
    return pl.pallas_call(
        functools.partial(attention_kernel, resident),
        out_shape=jax.ShapeDtypeStruct((group, BLOCK, width), jnp.bfloat16),
        in_specs=[SMEM, SMEM, SMEM, VMEM, VMEM, VMEM if resident else ANYWHERE],
        out_specs=VMEM,
        scratch_shapes=scratch,
        compiler_params=pltpu.CompilerParams(vmem_limit_bytes=ATTENTION_LIMIT),
        cost_estimate=SMALL,
        name="attention",
    )(jnp.full((1,), start, jnp.int32), slots, live, queries, output_weight, table)


def is_resident(shape):
    return 2 * math.prod(shape) <= RESIDENT


def by_time_kernel(where_ref, piece_ref, *refs):
    refs[-1][0] = piece_ref[...]


def by_time(where, piece, k, part, shape, earlier):
    operands, in_specs, aliases = [piece], [pl.BlockSpec(piece.shape, lambda i, w: (0, 0))], {}
    if earlier is not None:
        operands.append(earlier)
        in_specs.append(pl.BlockSpec(memory_space=pl.ANY))
        aliases = {2: 0}
    return pl.pallas_call(
        by_time_kernel,
        grid_spec=pltpu.PrefetchScalarGridSpec(
            num_scalar_prefetch=1,
            grid=(1,),
            in_specs=in_specs,
            out_specs=pl.BlockSpec((1,) + piece.shape, lambda i, w: (w[1] ^ k, part, 0)),
        ),
        out_shape=jax.ShapeDtypeStruct(shape, piece.dtype),
        input_output_aliases=aliases,
        compiler_params=pltpu.CompilerParams(vmem_limit_bytes=8 * MIB),
        cost_estimate=MEDIUM,
        name="by_time",
    )(where, *operands)


def shards(tokens, input_weight, output_weight, neighbours, degree):
    seg_dev, step_count, model_width = tokens.shape
    heads_here = lax.axis_size("head")
    regions = lax.axis_size("region")
    head_index = lax.axis_index("head")
    region_index = lax.axis_index("region")
    across = heads_here // step_count
    z = head_index // across
    x = head_index % across
    dev_blocks = seg_dev // BLOCK

    def z_move(piece, k):
        return lax.ppermute(
            piece, "head", [(i, i ^ (k * across)) for i in range(heads_here)]
        )

    def x_move(piece, k):
        return lax.ppermute(piece, "head", [(i, i ^ k) for i in range(heads_here)])

    def region_move(piece, k):
        return lax.ppermute(piece, "region", [(i, i ^ k) for i in range(regions)])

    where = jnp.stack([region_index, z, x]).astype(jnp.int32)
    places, slots, live = find_indices(
        where, neighbours, degree, across, dev_blocks, step_count
    )
    weight = sort_weight(input_weight)

    by_step = jnp.transpose(
        tokens.reshape(dev_blocks, CHUNKS, ROWS, step_count, model_width), (3, 1, 0, 2, 4)
    )
    to_send = [
        [lax.dynamic_index_in_dim(by_step[:, part], z ^ k, 0, keepdims=False)
         for k in range(step_count)]
        for part in range(CHUNKS)
    ]
    columns, pieces = {}, {}
    near, far = {}, {}
    region_blocks = dev_blocks * heads_here
    direct_first = region_blocks
    handed_first = region_blocks + (regions // 2 - 1) * BORDER
    table_blocks = region_blocks + (regions - 1) * BORDER
    split = CHUNKS // 2
    table, queries = None, None
    arrived, made = {}, {}
    z_pieces = {0: [z_move(piece, k + 1) for k, piece in enumerate(to_send[0][1:])]}

    def border_groups(part):
        row = part * ROWS
        if part < split:
            return [([piece[:BORDER] for piece in far[part]], direct_first, row)]
        by_region = [near[part]] + far[part]
        return [
            (by_region[1::2], direct_first, row),
            (by_region[0::2], handed_first, row),
        ]

    for turn in range(1, CHUNKS + 2):
        x_part, y_part = turn - 1, turn - 2
        held = {}
        if turn < CHUNKS:
            held["z"] = to_send[turn][1:]
        if x_part < CHUNKS:
            columns[x_part] = jnp.concatenate([to_send[x_part][0]] + z_pieces[x_part], axis=0)
            held["x"] = columns[x_part]
        if 0 <= y_part < split:
            near[y_part], *held["y"] = pick(
                places, pieces[y_part], [BORDER] + [2 * BORDER] * (regions // 2 - 1)
            )
        elif y_part >= split:
            held["y"] = pick(places, pieces[y_part], [BORDER] * (regions - 1))
        if turn == CHUNKS:
            held["core"] = jnp.concatenate(
                [
                    jnp.concatenate(
                        [near[part]] + [piece[BORDER:] for piece in far[part]], axis=0
                    )
                    for part in range(split)
                ],
                axis=1,
            )
        if turn == 1:
            made["index"] = (places, slots, live)
        if turn == 2:
            made["weight"] = weight
        held, made, arrived = lax.optimization_barrier((held, made, arrived))
        if turn == 1:
            places, slots, live = made["index"]
        weight = made.get("weight", weight)
        table, queries = made.get("table", (table, queries))
        made = {}
        groups = []
        if "x" in arrived:
            groups.append((pieces[turn - 2], 0, (turn - 2) * ROWS))
        if "y" in arrived:
            groups += border_groups(turn - 3)
        if "core" in arrived:
            groups.append(([arrived["core"]], handed_first, 0))
        if groups:
            made["table"] = project(
                weight, groups, table, table_blocks, queries, (turn - 2) * ROWS
            )
        arrived = {}
        if "x" in held:
            arrived["x"] = [x_move(held["x"], k) for k in range(1, across)]
            pieces[x_part] = [columns[x_part]] + arrived["x"]
        if "y" in held:
            if y_part < split:
                moved = [region_move(piece, 2 * (k + 1)) for k, piece in enumerate(held["y"])]
                far[y_part] = moved
            else:
                moved = [region_move(piece, k + 1) for k, piece in enumerate(held["y"])]
                near[y_part], *far[y_part] = moved
            arrived["y"] = moved
        if "core" in held:
            arrived["core"] = region_move(held["core"], 1)
        if "z" in held:
            z_pieces[turn] = [z_move(piece, k + 1) for k, piece in enumerate(held["z"])]
    table, queries = made["table"]
    (table,) = project(weight, border_groups(CHUNKS - 1), table, table_blocks)

    distances = [step_count - 1] + list(range(1, step_count - 1)) + [0]
    calls = [(k, block, 1) for k in distances for block in range(dev_blocks)]
    results = {}
    for k, block, count in calls:
        result = attention(
            k * dev_blocks + block, count, slots, live, queries, output_weight, table
        )
        slots, result = lax.optimization_barrier((slots, result))
        result = result.reshape(count * BLOCK, model_width)
        results[k, block, count] = z_move(result, k) if k else result
    stacked = None
    for k, block, count in calls[-dev_blocks:] + calls[:-dev_blocks]:
        stacked = by_time(
            where, results[k, block, count], k, block // count,
            (step_count, seg_dev, model_width), stacked,
        )
    return jnp.transpose(stacked, (1, 0, 2))


def solution(mesh):
    in_specs = (P(("region", "head"), None, None), P(), P(), P(), P())
    out_specs = P(("region", "head"), None, None)
    return jax.shard_map(shards, mesh=mesh, in_specs=in_specs, out_specs=out_specs, check_vma=False)
```

```python
import functools
import math

import jax
import jax.numpy as jnp
from jax import lax
from jax.experimental import pallas as pl
from jax.experimental.pallas import tpu as pltpu
from jax.sharding import PartitionSpec as P

HEADS = 16
HEAD_SIZE = 64
BLOCK = 128
SLOTS = 8
BORDER = 4
CHUNKS = 4
ROWS = BLOCK // CHUNKS
PAIR = 2 * HEAD_SIZE
UNROLL = 16
TILE = 512
MIB = 1024 * 1024
RESIDENT = 20 * MIB
PROJECT_LIMIT = 24 * MIB
ATTENTION_LIMIT = 24 * MIB
LOG2E = math.log2(math.e)
MEDIUM = pl.CostEstimate(flops=15 * 10**7, bytes_accessed=5 * 10**5, transcendentals=0)
SMALL = pl.CostEstimate(flops=1000, bytes_accessed=1000, transcendentals=0)

VMEM = pl.BlockSpec(memory_space=pltpu.VMEM)
SMEM = pl.BlockSpec(memory_space=pltpu.SMEM)
ANYWHERE = pl.BlockSpec(memory_space=pl.ANY)


def weight_kernel(in_ref, out_ref):
    rows, columns = out_ref.shape
    width = columns // 3
    low = lax.broadcasted_iota(jnp.int32, (rows, PAIR), 1) < HEAD_SIZE
    for pair in range(width // PAIR):
        one = in_ref[:, 3 * pair * PAIR : (3 * pair + 1) * PAIR]
        two = in_ref[:, (3 * pair + 1) * PAIR : (3 * pair + 2) * PAIR]
        three = in_ref[:, (3 * pair + 2) * PAIR : (3 * pair + 3) * PAIR]
        keys = jnp.concatenate([one[:, HEAD_SIZE:], three[:, :HEAD_SIZE]], axis=1)
        for number, value in enumerate(
            (keys, jnp.where(low, two, three), jnp.where(low, one, two))
        ):
            first = number * width + pair * PAIR
            out_ref[:, first : first + PAIR] = value


def sort_weight(weight):
    depth, columns = weight.shape
    rows = 128
    return pl.pallas_call(
        weight_kernel,
        grid=(depth // rows,),
        out_shape=jax.ShapeDtypeStruct((depth, columns), weight.dtype),
        in_specs=[pl.BlockSpec((rows, columns), lambda i: (i, 0))],
        out_specs=pl.BlockSpec((rows, columns), lambda i: (i, 0)),
        compiler_params=pltpu.CompilerParams(vmem_limit_bytes=8 * MIB),
        cost_estimate=SMALL,
        name="sort_weight",
    )(weight)


def index_kernel(
    across, dev_blocks, step_count, where_ref, list_ref, degree_ref,
    place_ref, slot_ref, live_ref, mark_ref, rank_ref,
):
    region, z, x = where_ref[0], where_ref[1], where_ref[2]
    blocks = list_ref.shape[0]
    region_blocks = across * dev_blocks * step_count
    column_blocks = dev_blocks * step_count
    regions = blocks // region_blocks

    def split(number, size):
        high = lax.div(number, jnp.int32(size))
        return high, number - high * size

    def home(local):
        owner, block = split(local, dev_blocks)
        owner_z, owner_x = split(owner, across)
        return (owner_x ^ x) * column_blocks + (owner_z ^ z) * dev_blocks + block

    def clear(i, carry):
        mark_ref[i] = 0
        rank_ref[i] = 0
        return carry

    lax.fori_loop(0, blocks, clear, 0, unroll=8)
    ours = region * region_blocks

    def look_from(namer, carry):
        base = namer * region_blocks

        def look(i, c):
            for slot in range(SLOTS):
                local = list_ref[base + i, slot] - ours
                inside = (local >= 0) & (local < region_blocks)
                mark_ref[jnp.where(inside, base + local, blocks)] = 1
            return c

        lax.fori_loop(0, region_blocks, look, 0)
        return carry

    lax.fori_loop(0, regions, look_from, 0)

    def look_here(i, carry):
        for slot in range(SLOTS):
            rank_ref[list_ref[ours + i, slot]] = 1
        return carry

    lax.fori_loop(0, region_blocks, look_here, 0)

    unused = (regions - 1) * BORDER

    def clear_places(i, carry):
        place_ref[i] = 0
        return carry

    lax.fori_loop(0, unused, clear_places, 0)

    def ranks(k, carry):
        base = (region ^ k) * region_blocks

        def one(local, counts):
            sent, got = counts
            marked = mark_ref[base + local]
            use = (marked == 1) & (sent < BORDER)
            place_ref[jnp.where(use, (k - 1) * BORDER + sent, unused)] = home(local)
            named = rank_ref[base + local]
            rank_ref[base + local] = got
            return sent + marked, got + named

        lax.fori_loop(0, region_blocks, one, (0, 0))
        return carry

    lax.fori_loop(1, regions, ranks, 0)

    def lists(i, carry):
        distance, block = split(i, dev_blocks)
        local = ((distance ^ z) * across + x) * dev_blocks + block
        live_ref[i] = degree_ref[ours + local]
        for slot in range(SLOTS):
            name = list_ref[ours + local, slot]
            name_region, name_local = split(name, region_blocks)
            source = name_region ^ region
            direct = ((source >> 1) - 1) * BORDER
            handed = (regions // 2 - 1 + (source >> 1)) * BORDER
            remote = region_blocks + jnp.where((source & 1) == 0, direct, handed) + rank_ref[name]
            slot_ref[i, slot] = jnp.where(source == 0, home(name_local), remote)
        return carry

    lax.fori_loop(0, column_blocks, lists, 0)


def find_indices(where, neighbours, degree, across, dev_blocks, step_count):
    blocks = neighbours.shape[0]
    region_blocks = across * dev_blocks * step_count
    regions = blocks // region_blocks
    column_blocks = dev_blocks * step_count
    return pl.pallas_call(
        functools.partial(index_kernel, across, dev_blocks, step_count),
        out_shape=[
            jax.ShapeDtypeStruct(((regions - 1) * BORDER + 1,), jnp.int32),
            jax.ShapeDtypeStruct((column_blocks, SLOTS), jnp.int32),
            jax.ShapeDtypeStruct((column_blocks,), jnp.int32),
        ],
        in_specs=[SMEM] * 3,
        out_specs=[SMEM] * 3,
        scratch_shapes=[pltpu.SMEM((blocks + 1,), jnp.int32), pltpu.SMEM((blocks + 1,), jnp.int32)],
        compiler_params=pltpu.CompilerParams(vmem_limit_bytes=1 * MIB),
        cost_estimate=SMALL,
        name="find_indices",
    )(where, neighbours, degree)


def project_kernel(groups, query, counts, *refs):
    total = sum(counts)
    weight_ref = refs[total]
    *outs, flat, stage, sems = refs
    if query is not None:
        *outs, q_ref = outs
    table_ref = outs[-1]
    width = table_ref.shape[2] // 2

    first = 0
    for piece in refs[:total]:
        rows = piece.shape[0] * piece.shape[1]
        flat[first : first + rows] = piece[...].reshape(rows, piece.shape[2])
        first += rows

    tiles = []
    for tile in range(0, 2 * width, TILE):
        targets = []
        first = 0
        for blocks, rows, first_block, first_row in groups:
            targets.append((first, blocks, rows, table_ref, first_block, first_row, tile))
            first += blocks * rows
        tiles.append((tile, first, targets))
    if query is not None:
        blocks, rows, first_row = query
        for tile in range(0, width, TILE):
            targets = [(0, blocks, rows, q_ref, 0, first_row, tile)]
            tiles.append((2 * width + tile, blocks * rows, targets))

    waiting = {0: [], 1: []}
    for number, (column, height, targets) in enumerate(tiles):
        slot = number % 2
        result = jnp.dot(
            flat[:height], weight_ref[:, column : column + TILE],
            preferred_element_type=jnp.float32,
        ).astype(jnp.bfloat16)
        for copy in waiting[slot]:
            copy.wait()
        waiting[slot] = []
        stage[slot, :height] = result
        for index, (first, blocks, rows, out_ref, first_block, first_row, tile) in enumerate(
            targets
        ):
            copy = pltpu.make_async_copy(
                stage.at[slot, pl.ds(first, blocks * rows), :].reshape(blocks, rows, TILE),
                out_ref.at[
                    pl.ds(first_block, blocks), pl.ds(first_row, rows), pl.ds(tile, TILE)
                ],
                sems.at[slot, index],
            )
            copy.start()
            waiting[slot].append(copy)
    for copies in waiting.values():
        for copy in copies:
            copy.wait()


def project(weight, groups, table, table_blocks, queries=None, query_row=None):
    depth, columns = weight.shape
    width = columns // 3
    operands, counts, shapes = [], [], []
    all_rows = 0
    for pieces, first_block, first_row in groups:
        blocks = sum(piece.shape[0] for piece in pieces)
        rows = pieces[0].shape[1]
        operands += pieces
        counts.append(len(pieces))
        shapes.append((blocks, rows, first_block, first_row))
        all_rows += blocks * rows
    operands.append(weight)
    in_specs = [VMEM] * len(operands)
    old = [table]
    out_shape = [jax.ShapeDtypeStruct((table_blocks, BLOCK, 2 * width), jnp.bfloat16)]
    query = None
    if query_row is not None:
        blocks, rows = groups[0][0][0].shape[:2]
        query = (blocks, rows, query_row)
        old.append(queries)
        out_shape.append(jax.ShapeDtypeStruct((blocks, BLOCK, width), jnp.bfloat16))
    aliases = {}
    for number, array in enumerate(old):
        if array is not None:
            aliases[len(operands)] = number
            operands.append(array)
            in_specs.append(ANYWHERE)
    return pl.pallas_call(
        functools.partial(project_kernel, tuple(shapes), query, tuple(counts)),
        out_shape=out_shape,
        in_specs=in_specs,
        out_specs=[ANYWHERE] * len(out_shape),
        scratch_shapes=[
            pltpu.VMEM((all_rows, depth), jnp.bfloat16),
            pltpu.VMEM((2, all_rows, TILE), jnp.bfloat16),
            pltpu.SemaphoreType.DMA((2, len(groups))),
        ],
        input_output_aliases=aliases,
        compiler_params=pltpu.CompilerParams(vmem_limit_bytes=PROJECT_LIMIT),
        cost_estimate=pl.CostEstimate(
            flops=4 * all_rows * depth * width, bytes_accessed=6 * all_rows * depth,
            transcendentals=0,
        ),
        name="project",
    )(*operands)


def pick_kernel(count, place_ref, *refs):
    pieces = refs[:count]
    part_blocks = pieces[0].shape[0]
    item = 0
    for out_ref in refs[count:]:
        for here in range(out_ref.shape[0]):
            place = place_ref[item]
            item += 1
            for index, piece in enumerate(pieces):

                @pl.when(place // part_blocks == index)
                def _():
                    out_ref[here] = piece[place % part_blocks]


def pick(places, pieces, counts):
    return pl.pallas_call(
        functools.partial(pick_kernel, len(pieces)),
        out_shape=[
            jax.ShapeDtypeStruct((count,) + pieces[0].shape[1:], pieces[0].dtype)
            for count in counts
        ],
        in_specs=[SMEM] + [VMEM] * len(pieces),
        out_specs=[VMEM] * len(counts),
        compiler_params=pltpu.CompilerParams(vmem_limit_bytes=8 * MIB),
        cost_estimate=SMALL,
        name="pick",
    )(places, *pieces)


def attend_block(slots, last_bias, width, load_q, load_kv, store):
    first = lax.broadcasted_iota(jnp.int32, (BLOCK, PAIR), 1) < HEAD_SIZE

    def one_pair(pair):
        columns = pl.ds(pl.multiple_of(pair * PAIR, PAIR), PAIR)
        values_at = pl.ds(pl.multiple_of(width + pair * PAIR, PAIR), PAIR)
        q = load_q(columns)
        zero = jnp.zeros_like(q)
        q_two = jnp.concatenate([jnp.where(first, q, zero), jnp.where(first, zero, q)], axis=0)
        keys = jnp.concatenate([load_kv(slot, columns) for slot in range(slots)], axis=0)
        values = jnp.concatenate([load_kv(slot, values_at) for slot in range(slots)], axis=0)
        scores = lax.dot_general(
            q_two, keys, (((1,), (1,)), ((), ())), preferred_element_type=jnp.float32
        )
        scores = jnp.concatenate([scores[:, :-BLOCK], scores[:, -BLOCK:] + last_bias], axis=1)
        top = jnp.max(scores, axis=1, keepdims=True)
        exponent = jnp.exp2((scores - top) * (HEAD_SIZE ** (-0.5) * LOG2E))
        total = jnp.sum(exponent, axis=1, keepdims=True)
        mixed = jnp.dot(
            exponent.astype(jnp.bfloat16), values, preferred_element_type=jnp.float32
        )
        mixed = mixed / total
        store(columns, jnp.where(first, mixed[:BLOCK], mixed[BLOCK:]).astype(jnp.bfloat16))

    pairs = math.gcd(width // PAIR, max(2, UNROLL // slots))

    def some_pairs(i, carry):
        for u in range(pairs):
            one_pair(i * pairs + u)
        return carry

    lax.fori_loop(0, width // PAIR // pairs, some_pairs, 0)


def attention_kernel(resident, start_ref, slot_ref, live_ref, q_ref, w_ref, table, out_ref, *scratch):
    group, _, width = out_ref.shape
    start = start_ref[0]
    att_buf = scratch[0]

    def place(block, slot):
        return slot_ref[block, jnp.where(slot < live_ref[block], slot, 0)]

    if not resident:
        kv_buf, sems = scratch[1:]

        def copies(block, action):
            def one(slot, carry):
                copy = pltpu.make_async_copy(
                    table.at[place(start + block, slot)], kv_buf.at[block, slot],
                    sems.at[block, slot],
                )
                if action == "start":
                    copy.start()
                else:
                    copy.wait()
                return carry

            lax.fori_loop(0, (live_ref[start + block] + 1) // 2 * 2, one, 0)

        for block in range(group):
            copies(block, "start")

    def one_block(block, carry):
        live = live_ref[start + block]
        if not resident:
            copies(block, "wait")

        def load_q(columns):
            return q_ref[start + block, :, columns]

        def load_kv(slot, columns):
            if resident:
                return table[place(start + block, slot), :, columns]
            return kv_buf[block, slot, :, columns]

        def store(columns, value):
            att_buf[block, :, columns] = value

        last_bias = jnp.where(live % 2 == 1, -jnp.inf, 0.0).astype(jnp.float32)
        for slots in range(2, SLOTS + 1, 2):

            @pl.when((live + 1) // 2 * 2 == slots)
            def _():
                attend_block(slots, last_bias, width, load_q, load_kv, store)

        return carry

    lax.fori_loop(0, group, one_block, 0)
    flat = att_buf[...].reshape(group * BLOCK, width)

    def one_tile(tile, carry):
        here = pl.ds(pl.multiple_of(tile * TILE, TILE), TILE)
        out_ref[:, :, here] = (
            jnp.dot(flat, w_ref[:, here], preferred_element_type=jnp.float32)
            .astype(jnp.bfloat16)
            .reshape(group, BLOCK, TILE)
        )
        return carry

    lax.fori_loop(0, width // TILE, one_tile, 0)


def attention(start, group, slots, live, queries, output_weight, table):
    width = queries.shape[2]
    resident = is_resident(table.shape)
    scratch = [pltpu.VMEM((group, BLOCK, width), jnp.bfloat16)]
    if not resident:
        scratch += [
            pltpu.VMEM((group, SLOTS, BLOCK, 2 * width), jnp.bfloat16),
            pltpu.SemaphoreType.DMA((group, SLOTS)),
        ]
    return pl.pallas_call(
        functools.partial(attention_kernel, resident),
        out_shape=jax.ShapeDtypeStruct((group, BLOCK, width), jnp.bfloat16),
        in_specs=[SMEM, SMEM, SMEM, VMEM, VMEM, VMEM if resident else ANYWHERE],
        out_specs=VMEM,
        scratch_shapes=scratch,
        compiler_params=pltpu.CompilerParams(vmem_limit_bytes=ATTENTION_LIMIT),
        cost_estimate=SMALL,
        name="attention",
    )(jnp.full((1,), start, jnp.int32), slots, live, queries, output_weight, table)


def is_resident(shape):
    return 2 * math.prod(shape) <= RESIDENT


def by_time_kernel(count, where_ref, *refs):
    out_ref = refs[-1]
    rows = refs[0].shape[0]
    for index in range(count):
        out_ref[0, index * rows : (index + 1) * rows] = refs[index][...]


def by_time(where, pieces, k, part, shape, earlier):
    count = len(pieces)
    rows, width = pieces[0].shape
    operands = list(pieces)
    in_specs = [pl.BlockSpec((rows, width), lambda i, w: (0, 0))] * count
    aliases = {}
    if earlier is not None:
        operands.append(earlier)
        in_specs.append(ANYWHERE)
        aliases = {1 + count: 0}
    return pl.pallas_call(
        functools.partial(by_time_kernel, count),
        grid_spec=pltpu.PrefetchScalarGridSpec(
            num_scalar_prefetch=1,
            grid=(1,),
            in_specs=in_specs,
            out_specs=pl.BlockSpec((1, count * rows, width), lambda i, w: (w[1] ^ k, part, 0)),
        ),
        out_shape=jax.ShapeDtypeStruct(shape, pieces[0].dtype),
        input_output_aliases=aliases,
        compiler_params=pltpu.CompilerParams(vmem_limit_bytes=8 * MIB),
        cost_estimate=MEDIUM,
        name="by_time",
    )(where, *operands)


def shards(tokens, input_weight, output_weight, neighbours, degree):
    seg_dev, step_count, model_width = tokens.shape
    heads_here = lax.axis_size("head")
    regions = lax.axis_size("region")
    head_index = lax.axis_index("head")
    region_index = lax.axis_index("region")
    across = heads_here // step_count
    z = head_index // across
    x = head_index % across
    dev_blocks = seg_dev // BLOCK

    def z_move(piece, k):
        return lax.ppermute(
            piece, "head", [(i, i ^ (k * across)) for i in range(heads_here)]
        )

    def x_move(piece, k):
        return lax.ppermute(piece, "head", [(i, i ^ k) for i in range(heads_here)])

    def region_move(piece, k):
        return lax.ppermute(piece, "region", [(i, i ^ k) for i in range(regions)])

    where = jnp.stack([region_index, z, x]).astype(jnp.int32)
    places, slots, live = find_indices(
        where, neighbours, degree, across, dev_blocks, step_count
    )
    weight = sort_weight(input_weight)

    by_step = jnp.transpose(
        tokens.reshape(dev_blocks, CHUNKS, ROWS, step_count, model_width), (3, 1, 0, 2, 4)
    )
    to_send = [
        [lax.dynamic_index_in_dim(by_step[:, part], z ^ k, 0, keepdims=False)
         for k in range(step_count)]
        for part in range(CHUNKS)
    ]
    columns, pieces = {}, {}
    near, far = {}, {}
    region_blocks = dev_blocks * heads_here
    direct_first = region_blocks
    handed_first = region_blocks + (regions // 2 - 1) * BORDER
    table_blocks = region_blocks + (regions - 1) * BORDER
    split = CHUNKS // 2
    table, queries = None, None
    arrived, made = {}, {}
    z_pieces = {0: [z_move(piece, k + 1) for k, piece in enumerate(to_send[0][1:])]}

    def border_groups(part):
        row = part * ROWS
        if part < split:
            return [([piece[:BORDER] for piece in far[part]], direct_first, row)]
        by_region = [near[part]] + far[part]
        return [
            (by_region[1::2], direct_first, row),
            (by_region[0::2], handed_first, row),
        ]

    for turn in range(1, CHUNKS + 2):
        x_part, y_part = turn - 1, turn - 2
        held = {}
        if turn < CHUNKS:
            held["z"] = to_send[turn][1:]
        if x_part < CHUNKS:
            columns[x_part] = jnp.concatenate([to_send[x_part][0]] + z_pieces[x_part], axis=0)
            held["x"] = columns[x_part]
        if 0 <= y_part < split:
            near[y_part], *held["y"] = pick(
                places, pieces[y_part], [BORDER] + [2 * BORDER] * (regions // 2 - 1)
            )
        elif y_part >= split:
            held["y"] = pick(places, pieces[y_part], [BORDER] * (regions - 1))
        if turn == CHUNKS:
            held["core"] = jnp.concatenate(
                [
                    jnp.concatenate(
                        [near[part]] + [piece[BORDER:] for piece in far[part]], axis=0
                    )
                    for part in range(split)
                ],
                axis=1,
            )
        if turn == 1:
            made["index"] = (places, slots, live)
        if turn == 2:
            made["weight"] = weight
        held, made, arrived = lax.optimization_barrier((held, made, arrived))
        if turn == 1:
            places, slots, live = made["index"]
        weight = made.get("weight", weight)
        table, queries = made.get("table", (table, queries))
        made = {}
        groups = []
        if "x" in arrived:
            groups.append((pieces[turn - 2], 0, (turn - 2) * ROWS))
        if "y" in arrived:
            groups += border_groups(turn - 3)
        if "core" in arrived:
            groups.append(([arrived["core"]], handed_first, 0))
        if groups:
            made["table"] = project(
                weight, groups, table, table_blocks, queries, (turn - 2) * ROWS
            )
        arrived = {}
        if "x" in held:
            arrived["x"] = [x_move(held["x"], k) for k in range(1, across)]
            pieces[x_part] = [columns[x_part]] + arrived["x"]
        if "y" in held:
            if y_part < split:
                moved = [region_move(piece, 2 * (k + 1)) for k, piece in enumerate(held["y"])]
                far[y_part] = moved
            else:
                moved = [region_move(piece, k + 1) for k, piece in enumerate(held["y"])]
                near[y_part], *far[y_part] = moved
            arrived["y"] = moved
        if "core" in held:
            arrived["core"] = region_move(held["core"], 1)
        if "z" in held:
            z_pieces[turn] = [z_move(piece, k + 1) for k, piece in enumerate(held["z"])]
    table, queries = made["table"]
    (table,) = project(weight, border_groups(CHUNKS - 1), table, table_blocks)

    distances = [step_count - 1] + list(range(1, step_count - 1)) + [0]
    calls = [(k, block, 1) for k in distances for block in range(dev_blocks)]
    results = {}
    for k, block, count in calls:
        result = attention(
            k * dev_blocks + block, count, slots, live, queries, output_weight, table
        )
        slots, result = lax.optimization_barrier((slots, result))
        result = result.reshape(count * BLOCK, model_width)
        results[k, block, count] = z_move(result, k) if k else result
    own = [results.pop((0, block, 1)) for block in range(dev_blocks)]
    stacked = by_time(
        where, own, 0, 0, (step_count, seg_dev, model_width), None
    )
    for k, block, count in calls[:-dev_blocks]:
        stacked = by_time(
            where, [results[k, block, count]], k, block // count,
            (step_count, seg_dev, model_width), stacked,
        )
    return jnp.transpose(stacked, (1, 0, 2))


def solution(mesh):
    in_specs = (P(("region", "head"), None, None), P(), P(), P(), P())
    out_specs = P(("region", "head"), None, None)
    return jax.shard_map(shards, mesh=mesh, in_specs=in_specs, out_specs=out_specs, check_vma=False)
```

```python
import functools
import math

import jax
import jax.numpy as jnp
from jax import lax
from jax.experimental import pallas as pl
from jax.experimental.pallas import tpu as pltpu
from jax.sharding import PartitionSpec as P

HEADS = 16
HEAD_SIZE = 64
BLOCK = 128
SLOTS = 8
BORDER = 4
CHUNKS = 4
ROWS = BLOCK // CHUNKS
PAIR = 2 * HEAD_SIZE
UNROLL = 16
TILE = 512
MIB = 1024 * 1024
RESIDENT = 20 * MIB
PROJECT_LIMIT = 24 * MIB
ATTENTION_LIMIT = 24 * MIB
LOG2E = math.log2(math.e)
MEDIUM = pl.CostEstimate(flops=15 * 10**7, bytes_accessed=5 * 10**5, transcendentals=0)
SMALL = pl.CostEstimate(flops=1000, bytes_accessed=1000, transcendentals=0)

VMEM = pl.BlockSpec(memory_space=pltpu.VMEM)
SMEM = pl.BlockSpec(memory_space=pltpu.SMEM)
ANYWHERE = pl.BlockSpec(memory_space=pl.ANY)


def weight_kernel(in_ref, out_ref):
    rows, columns = out_ref.shape
    width = columns // 3
    low = lax.broadcasted_iota(jnp.int32, (rows, PAIR), 1) < HEAD_SIZE
    for pair in range(width // PAIR):
        one = in_ref[:, 3 * pair * PAIR : (3 * pair + 1) * PAIR]
        two = in_ref[:, (3 * pair + 1) * PAIR : (3 * pair + 2) * PAIR]
        three = in_ref[:, (3 * pair + 2) * PAIR : (3 * pair + 3) * PAIR]
        keys = jnp.concatenate([one[:, HEAD_SIZE:], three[:, :HEAD_SIZE]], axis=1)
        for number, value in enumerate(
            (keys, jnp.where(low, two, three), jnp.where(low, one, two))
        ):
            first = number * width + pair * PAIR
            out_ref[:, first : first + PAIR] = value


def sort_weight(weight):
    depth, columns = weight.shape
    rows = 128
    return pl.pallas_call(
        weight_kernel,
        grid=(depth // rows,),
        out_shape=jax.ShapeDtypeStruct((depth, columns), weight.dtype),
        in_specs=[pl.BlockSpec((rows, columns), lambda i: (i, 0))],
        out_specs=pl.BlockSpec((rows, columns), lambda i: (i, 0)),
        compiler_params=pltpu.CompilerParams(vmem_limit_bytes=8 * MIB),
        cost_estimate=SMALL,
        name="sort_weight",
    )(weight)


def index_kernel(
    across, dev_blocks, step_count, where_ref, list_ref, degree_ref,
    place_ref, slot_ref, live_ref, mark_ref, rank_ref,
):
    region, z, x = where_ref[0], where_ref[1], where_ref[2]
    blocks = list_ref.shape[0]
    region_blocks = across * dev_blocks * step_count
    column_blocks = dev_blocks * step_count
    regions = blocks // region_blocks

    def split(number, size):
        high = lax.div(number, jnp.int32(size))
        return high, number - high * size

    def home(local):
        owner, block = split(local, dev_blocks)
        owner_z, owner_x = split(owner, across)
        return (owner_x ^ x) * column_blocks + (owner_z ^ z) * dev_blocks + block

    def clear(i, carry):
        mark_ref[i] = 0
        rank_ref[i] = 0
        return carry

    lax.fori_loop(0, blocks, clear, 0, unroll=8)
    ours = region * region_blocks

    def look_from(namer, carry):
        base = namer * region_blocks

        def look(i, c):
            for slot in range(SLOTS):
                local = list_ref[base + i, slot] - ours
                inside = (local >= 0) & (local < region_blocks)
                mark_ref[jnp.where(inside, base + local, blocks)] = 1
            return c

        lax.fori_loop(0, region_blocks, look, 0)
        return carry

    lax.fori_loop(0, regions, look_from, 0)

    def look_here(i, carry):
        for slot in range(SLOTS):
            rank_ref[list_ref[ours + i, slot]] = 1
        return carry

    lax.fori_loop(0, region_blocks, look_here, 0)

    unused = (regions - 1) * BORDER

    def clear_places(i, carry):
        place_ref[i] = 0
        return carry

    lax.fori_loop(0, unused, clear_places, 0)

    def ranks(k, carry):
        base = (region ^ k) * region_blocks

        def one(local, counts):
            sent, got = counts
            marked = mark_ref[base + local]
            use = (marked == 1) & (sent < BORDER)
            place_ref[jnp.where(use, (k - 1) * BORDER + sent, unused)] = home(local)
            named = rank_ref[base + local]
            rank_ref[base + local] = got
            return sent + marked, got + named

        lax.fori_loop(0, region_blocks, one, (0, 0))
        return carry

    lax.fori_loop(1, regions, ranks, 0)

    def lists(i, carry):
        distance, block = split(i, dev_blocks)
        local = ((distance ^ z) * across + x) * dev_blocks + block
        live_ref[i] = degree_ref[ours + local]
        for slot in range(SLOTS):
            name = list_ref[ours + local, slot]
            name_region, name_local = split(name, region_blocks)
            source = name_region ^ region
            direct = ((source >> 1) - 1) * BORDER
            handed = (regions // 2 - 1 + (source >> 1)) * BORDER
            remote = region_blocks + jnp.where((source & 1) == 0, direct, handed) + rank_ref[name]
            slot_ref[i, slot] = jnp.where(source == 0, home(name_local), remote)
        return carry

    lax.fori_loop(0, column_blocks, lists, 0)


def find_indices(where, neighbours, degree, across, dev_blocks, step_count):
    blocks = neighbours.shape[0]
    region_blocks = across * dev_blocks * step_count
    regions = blocks // region_blocks
    column_blocks = dev_blocks * step_count
    return pl.pallas_call(
        functools.partial(index_kernel, across, dev_blocks, step_count),
        out_shape=[
            jax.ShapeDtypeStruct(((regions - 1) * BORDER + 1,), jnp.int32),
            jax.ShapeDtypeStruct((column_blocks, SLOTS), jnp.int32),
            jax.ShapeDtypeStruct((column_blocks,), jnp.int32),
        ],
        in_specs=[SMEM] * 3,
        out_specs=[SMEM] * 3,
        scratch_shapes=[pltpu.SMEM((blocks + 1,), jnp.int32), pltpu.SMEM((blocks + 1,), jnp.int32)],
        compiler_params=pltpu.CompilerParams(vmem_limit_bytes=1 * MIB),
        cost_estimate=SMALL,
        name="find_indices",
    )(where, neighbours, degree)


def project_kernel(groups, query, counts, *refs):
    total = sum(counts)
    weight_ref = refs[total]
    *outs, flat, stage, sems = refs
    if query is not None:
        *outs, q_ref = outs
    table_ref = outs[-1]
    width = table_ref.shape[2] // 2

    first = 0
    for piece in refs[:total]:
        rows = piece.shape[0] * piece.shape[1]
        flat[first : first + rows] = piece[...].reshape(rows, piece.shape[2])
        first += rows

    tiles = []
    for tile in range(0, 2 * width, TILE):
        targets = []
        first = 0
        for blocks, rows, first_block, first_row in groups:
            targets.append((first, blocks, rows, table_ref, first_block, first_row, tile))
            first += blocks * rows
        tiles.append((tile, first, targets))
    if query is not None:
        blocks, rows, first_row = query
        for tile in range(0, width, TILE):
            targets = [(0, blocks, rows, q_ref, 0, first_row, tile)]
            tiles.append((2 * width + tile, blocks * rows, targets))

    waiting = {0: [], 1: []}
    for number, (column, height, targets) in enumerate(tiles):
        slot = number % 2
        result = jnp.dot(
            flat[:height], weight_ref[:, column : column + TILE],
            preferred_element_type=jnp.float32,
        ).astype(jnp.bfloat16)
        for copy in waiting[slot]:
            copy.wait()
        waiting[slot] = []
        stage[slot, :height] = result
        for index, (first, blocks, rows, out_ref, first_block, first_row, tile) in enumerate(
            targets
        ):
            copy = pltpu.make_async_copy(
                stage.at[slot, pl.ds(first, blocks * rows), :].reshape(blocks, rows, TILE),
                out_ref.at[
                    pl.ds(first_block, blocks), pl.ds(first_row, rows), pl.ds(tile, TILE)
                ],
                sems.at[slot, index],
            )
            copy.start()
            waiting[slot].append(copy)
    for copies in waiting.values():
        for copy in copies:
            copy.wait()


def project(weight, groups, table, table_blocks, queries=None, query_row=None):
    depth, columns = weight.shape
    width = columns // 3
    operands, counts, shapes = [], [], []
    all_rows = 0
    for pieces, first_block, first_row in groups:
        blocks = sum(piece.shape[0] for piece in pieces)
        rows = pieces[0].shape[1]
        operands += pieces
        counts.append(len(pieces))
        shapes.append((blocks, rows, first_block, first_row))
        all_rows += blocks * rows
    operands.append(weight)
    in_specs = [VMEM] * len(operands)
    old = [table]
    out_shape = [jax.ShapeDtypeStruct((table_blocks, BLOCK, 2 * width), jnp.bfloat16)]
    query = None
    if query_row is not None:
        blocks, rows = groups[0][0][0].shape[:2]
        query = (blocks, rows, query_row)
        old.append(queries)
        out_shape.append(jax.ShapeDtypeStruct((blocks, BLOCK, width), jnp.bfloat16))
    aliases = {}
    for number, array in enumerate(old):
        if array is not None:
            aliases[len(operands)] = number
            operands.append(array)
            in_specs.append(ANYWHERE)
    return pl.pallas_call(
        functools.partial(project_kernel, tuple(shapes), query, tuple(counts)),
        out_shape=out_shape,
        in_specs=in_specs,
        out_specs=[ANYWHERE] * len(out_shape),
        scratch_shapes=[
            pltpu.VMEM((all_rows, depth), jnp.bfloat16),
            pltpu.VMEM((2, all_rows, TILE), jnp.bfloat16),
            pltpu.SemaphoreType.DMA((2, len(groups))),
        ],
        input_output_aliases=aliases,
        compiler_params=pltpu.CompilerParams(vmem_limit_bytes=PROJECT_LIMIT),
        cost_estimate=pl.CostEstimate(
            flops=4 * all_rows * depth * width, bytes_accessed=6 * all_rows * depth,
            transcendentals=0,
        ),
        name="project",
    )(*operands)


def pick_kernel(count, place_ref, *refs):
    pieces = refs[:count]
    part_blocks = pieces[0].shape[0]
    item = 0
    for out_ref in refs[count:]:
        for here in range(out_ref.shape[0]):
            place = place_ref[item]
            item += 1
            for index, piece in enumerate(pieces):

                @pl.when(place // part_blocks == index)
                def _():
                    out_ref[here] = piece[place % part_blocks]


def pick(places, pieces, counts):
    return pl.pallas_call(
        functools.partial(pick_kernel, len(pieces)),
        out_shape=[
            jax.ShapeDtypeStruct((count,) + pieces[0].shape[1:], pieces[0].dtype)
            for count in counts
        ],
        in_specs=[SMEM] + [VMEM] * len(pieces),
        out_specs=[VMEM] * len(counts),
        compiler_params=pltpu.CompilerParams(vmem_limit_bytes=8 * MIB),
        cost_estimate=SMALL,
        name="pick",
    )(places, *pieces)


def attend_block(slots, last_bias, width, load_q, load_kv, store):
    first = lax.broadcasted_iota(jnp.int32, (BLOCK, PAIR), 1) < HEAD_SIZE

    def one_pair(pair):
        columns = pl.ds(pl.multiple_of(pair * PAIR, PAIR), PAIR)
        values_at = pl.ds(pl.multiple_of(width + pair * PAIR, PAIR), PAIR)
        q = load_q(columns)
        zero = jnp.zeros_like(q)
        q_two = jnp.concatenate([jnp.where(first, q, zero), jnp.where(first, zero, q)], axis=0)
        keys = jnp.concatenate([load_kv(slot, columns) for slot in range(slots)], axis=0)
        values = jnp.concatenate([load_kv(slot, values_at) for slot in range(slots)], axis=0)
        scores = lax.dot_general(
            q_two, keys, (((1,), (1,)), ((), ())), preferred_element_type=jnp.float32
        )
        scores = jnp.concatenate([scores[:, :-BLOCK], scores[:, -BLOCK:] + last_bias], axis=1)
        top = jnp.max(scores, axis=1, keepdims=True)
        exponent = jnp.exp2((scores - top) * (HEAD_SIZE ** (-0.5) * LOG2E))
        total = jnp.sum(exponent, axis=1, keepdims=True)
        mixed = jnp.dot(
            exponent.astype(jnp.bfloat16), values, preferred_element_type=jnp.float32
        )
        mixed = mixed / total
        store(columns, jnp.where(first, mixed[:BLOCK], mixed[BLOCK:]).astype(jnp.bfloat16))

    pairs = math.gcd(width // PAIR, max(4, UNROLL // slots))

    def some_pairs(i, carry):
        for u in range(pairs):
            one_pair(i * pairs + u)
        return carry

    lax.fori_loop(0, width // PAIR // pairs, some_pairs, 0)


def attention_kernel(resident, start_ref, slot_ref, live_ref, q_ref, w_ref, table, out_ref, *scratch):
    group, _, width = out_ref.shape
    start = start_ref[0]
    att_buf = scratch[0]

    def place(block, slot):
        return slot_ref[block, jnp.where(slot < live_ref[block], slot, 0)]

    if not resident:
        kv_buf, sems = scratch[1:]

        def copies(block, action):
            def one(slot, carry):
                copy = pltpu.make_async_copy(
                    table.at[place(start + block, slot)], kv_buf.at[block, slot],
                    sems.at[block, slot],
                )
                if action == "start":
                    copy.start()
                else:
                    copy.wait()
                return carry

            lax.fori_loop(0, (live_ref[start + block] + 1) // 2 * 2, one, 0)

        for block in range(group):
            copies(block, "start")

    def one_block(block, carry):
        live = live_ref[start + block]
        if not resident:
            copies(block, "wait")

        def load_q(columns):
            return q_ref[start + block, :, columns]

        def load_kv(slot, columns):
            if resident:
                return table[place(start + block, slot), :, columns]
            return kv_buf[block, slot, :, columns]

        def store(columns, value):
            att_buf[block, :, columns] = value

        last_bias = jnp.where(live % 2 == 1, -jnp.inf, 0.0).astype(jnp.float32)
        for slots in range(2, SLOTS + 1, 2):

            @pl.when((live + 1) // 2 * 2 == slots)
            def _():
                attend_block(slots, last_bias, width, load_q, load_kv, store)

        return carry

    lax.fori_loop(0, group, one_block, 0)
    flat = att_buf[...].reshape(group * BLOCK, width)

    def one_tile(tile, carry):
        here = pl.ds(pl.multiple_of(tile * TILE, TILE), TILE)
        out_ref[:, :, here] = (
            jnp.dot(flat, w_ref[:, here], preferred_element_type=jnp.float32)
            .astype(jnp.bfloat16)
            .reshape(group, BLOCK, TILE)
        )
        return carry

    lax.fori_loop(0, width // TILE, one_tile, 0)


def attention(start, group, slots, live, queries, output_weight, table):
    width = queries.shape[2]
    resident = is_resident(table.shape)
    scratch = [pltpu.VMEM((group, BLOCK, width), jnp.bfloat16)]
    if not resident:
        scratch += [
            pltpu.VMEM((group, SLOTS, BLOCK, 2 * width), jnp.bfloat16),
            pltpu.SemaphoreType.DMA((group, SLOTS)),
        ]
    return pl.pallas_call(
        functools.partial(attention_kernel, resident),
        out_shape=jax.ShapeDtypeStruct((group, BLOCK, width), jnp.bfloat16),
        in_specs=[SMEM, SMEM, SMEM, VMEM, VMEM, VMEM if resident else ANYWHERE],
        out_specs=VMEM,
        scratch_shapes=scratch,
        compiler_params=pltpu.CompilerParams(vmem_limit_bytes=ATTENTION_LIMIT),
        cost_estimate=SMALL,
        name="attention",
    )(jnp.full((1,), start, jnp.int32), slots, live, queries, output_weight, table)


def is_resident(shape):
    return 2 * math.prod(shape) <= RESIDENT


def by_time_kernel(count, where_ref, *refs):
    out_ref = refs[-1]
    rows = refs[0].shape[0]
    for index in range(count):
        out_ref[0, index * rows : (index + 1) * rows] = refs[index][...]


def by_time(where, pieces, k, part, shape, earlier):
    count = len(pieces)
    rows, width = pieces[0].shape
    operands = list(pieces)
    in_specs = [pl.BlockSpec((rows, width), lambda i, w: (0, 0))] * count
    aliases = {}
    if earlier is not None:
        operands.append(earlier)
        in_specs.append(ANYWHERE)
        aliases = {1 + count: 0}
    return pl.pallas_call(
        functools.partial(by_time_kernel, count),
        grid_spec=pltpu.PrefetchScalarGridSpec(
            num_scalar_prefetch=1,
            grid=(1,),
            in_specs=in_specs,
            out_specs=pl.BlockSpec((1, count * rows, width), lambda i, w: (w[1] ^ k, part, 0)),
        ),
        out_shape=jax.ShapeDtypeStruct(shape, pieces[0].dtype),
        input_output_aliases=aliases,
        compiler_params=pltpu.CompilerParams(vmem_limit_bytes=8 * MIB),
        cost_estimate=MEDIUM,
        name="by_time",
    )(where, *operands)


def shards(tokens, input_weight, output_weight, neighbours, degree):
    seg_dev, step_count, model_width = tokens.shape
    heads_here = lax.axis_size("head")
    regions = lax.axis_size("region")
    head_index = lax.axis_index("head")
    region_index = lax.axis_index("region")
    across = heads_here // step_count
    z = head_index // across
    x = head_index % across
    dev_blocks = seg_dev // BLOCK

    def z_move(piece, k):
        return lax.ppermute(
            piece, "head", [(i, i ^ (k * across)) for i in range(heads_here)]
        )

    def x_move(piece, k):
        return lax.ppermute(piece, "head", [(i, i ^ k) for i in range(heads_here)])

    def region_move(piece, k):
        return lax.ppermute(piece, "region", [(i, i ^ k) for i in range(regions)])

    where = jnp.stack([region_index, z, x]).astype(jnp.int32)
    places, slots, live = find_indices(
        where, neighbours, degree, across, dev_blocks, step_count
    )
    weight = sort_weight(input_weight)

    by_step = jnp.transpose(
        tokens.reshape(dev_blocks, CHUNKS, ROWS, step_count, model_width), (3, 1, 0, 2, 4)
    )
    to_send = [
        [lax.dynamic_index_in_dim(by_step[:, part], z ^ k, 0, keepdims=False)
         for k in range(step_count)]
        for part in range(CHUNKS)
    ]
    columns, pieces = {}, {}
    near, far = {}, {}
    region_blocks = dev_blocks * heads_here
    direct_first = region_blocks
    handed_first = region_blocks + (regions // 2 - 1) * BORDER
    table_blocks = region_blocks + (regions - 1) * BORDER
    split = CHUNKS // 2
    table, queries = None, None
    arrived, made = {}, {}
    z_pieces = {0: [z_move(piece, k + 1) for k, piece in enumerate(to_send[0][1:])]}

    def border_groups(part):
        row = part * ROWS
        if part < split:
            return [([piece[:BORDER] for piece in far[part]], direct_first, row)]
        by_region = [near[part]] + far[part]
        return [
            (by_region[1::2], direct_first, row),
            (by_region[0::2], handed_first, row),
        ]

    for turn in range(1, CHUNKS + 2):
        x_part, y_part = turn - 1, turn - 2
        held = {}
        if turn < CHUNKS:
            held["z"] = to_send[turn][1:]
        if x_part < CHUNKS:
            columns[x_part] = jnp.concatenate([to_send[x_part][0]] + z_pieces[x_part], axis=0)
            held["x"] = columns[x_part]
        if 0 <= y_part < split:
            near[y_part], *held["y"] = pick(
                places, pieces[y_part], [BORDER] + [2 * BORDER] * (regions // 2 - 1)
            )
        elif y_part >= split:
            held["y"] = pick(places, pieces[y_part], [BORDER] * (regions - 1))
        if turn == CHUNKS:
            held["core"] = jnp.concatenate(
                [
                    jnp.concatenate(
                        [near[part]] + [piece[BORDER:] for piece in far[part]], axis=0
                    )
                    for part in range(split)
                ],
                axis=1,
            )
        if turn == 1:
            made["index"] = (places, slots, live)
        if turn == 2:
            made["weight"] = weight
        held, made, arrived = lax.optimization_barrier((held, made, arrived))
        if turn == 1:
            places, slots, live = made["index"]
        weight = made.get("weight", weight)
        table, queries = made.get("table", (table, queries))
        made = {}
        groups = []
        if "x" in arrived:
            groups.append((pieces[turn - 2], 0, (turn - 2) * ROWS))
        if "y" in arrived:
            groups += border_groups(turn - 3)
        if "core" in arrived:
            groups.append(([arrived["core"]], handed_first, 0))
        if groups:
            made["table"] = project(
                weight, groups, table, table_blocks, queries, (turn - 2) * ROWS
            )
        arrived = {}
        if "x" in held:
            arrived["x"] = [x_move(held["x"], k) for k in range(1, across)]
            pieces[x_part] = [columns[x_part]] + arrived["x"]
        if "y" in held:
            if y_part < split:
                moved = [region_move(piece, 2 * (k + 1)) for k, piece in enumerate(held["y"])]
                far[y_part] = moved
            else:
                moved = [region_move(piece, k + 1) for k, piece in enumerate(held["y"])]
                near[y_part], *far[y_part] = moved
            arrived["y"] = moved
        if "core" in held:
            arrived["core"] = region_move(held["core"], 1)
        if "z" in held:
            z_pieces[turn] = [z_move(piece, k + 1) for k, piece in enumerate(held["z"])]
    table, queries = made["table"]
    (table,) = project(weight, border_groups(CHUNKS - 1), table, table_blocks)

    distances = [step_count - 1] + list(range(1, step_count - 1)) + [0]
    calls = [(k, block, 1) for k in distances for block in range(dev_blocks)]
    results = {}
    for k, block, count in calls:
        result = attention(
            k * dev_blocks + block, count, slots, live, queries, output_weight, table
        )
        slots, result = lax.optimization_barrier((slots, result))
        result = result.reshape(count * BLOCK, model_width)
        results[k, block, count] = z_move(result, k) if k else result
    own = [results.pop((0, block, 1)) for block in range(dev_blocks)]
    stacked = by_time(
        where, own, 0, 0, (step_count, seg_dev, model_width), None
    )
    for k, block, count in calls[:-dev_blocks]:
        stacked = by_time(
            where, [results[k, block, count]], k, block // count,
            (step_count, seg_dev, model_width), stacked,
        )
    return jnp.transpose(stacked, (1, 0, 2))


def solution(mesh):
    in_specs = (P(("region", "head"), None, None), P(), P(), P(), P())
    out_specs = P(("region", "head"), None, None)
    return jax.shard_map(shards, mesh=mesh, in_specs=in_specs, out_specs=out_specs, check_vma=False)
```
